512 devices in a mesh: res: 128 (over z, y, core), crop: 4 (over x).
Axes of the slice: x: 4, y: 8, z: 8, core: 2. Of those that a mesh axis runs over, the one named last changes fastest.
Arguments:
- pair_input: bfloat16 [2560, 640, 128], P(('crop', 'res')), parts along dimension 0, may hold values from -40 to 40
- gain_in: float32 [128], replicated, may hold values from 0.5 to 1.5
- w_in: bfloat16 [128, 640], replicated, may hold values from -0.5 to 0.5
- w_out: bfloat16 [128, 128], replicated, may hold values from -0.5 to 0.5
- product_gain: float32 [128], replicated, may hold values from 0.5 to 1.5
- cotangent: bfloat16 [2560, 640, 128], P(('crop', 'res')), parts along dimension 0, may hold values from -6 to 6
Outputs:
- update: bfloat16 [2560, 640, 128], P(('crop', 'res')), parts along dimension 0
- grad_pair: bfloat16 [2560, 640, 128], P(('crop', 'res')), parts along dimension 0
- grad_w_in: float32 [512, 640], P('crop'), parts along dimension 0
- grad_w_out: float32 [512, 128], P('crop'), parts along dimension 0
- grad_gain_in: float32 [512], P('crop'), parts along dimension 0
- grad_gain_out: float32 [512], P('crop'), parts along dimension 0
The draws below stay inside these ranges and needn't reach their ends.
There are 4 independent parts, one for each index of `crop`. The reference program is written for one: setup_inputs(seed, part) draws one part's arguments, and reference() takes and returns one part's arrays. A program takes and returns all parts, laid end to end along the dimension named above; an argument that names none is the same for every part. Nothing has to cross between parts.
All inputs are finite; a program needn't handle non-finite values.
Results may differ from the reference program's by a relative error of at most 0.0085.
Values may be sent and summed in bfloat16 or wider, within the bound.
A program may use at most 64 MiB of HBM per device.

```python
import jax
import jax.numpy as jnp
from jax import lax

C = 128
N = 640


def draw_pair_input(key, part):
    key = jax.random.fold_in(key, 11)
    first, second, third = jax.random.split(key, 3)
    channel_scale = jnp.exp(jax.random.uniform(second, (C,), minval=-1.15, maxval=1.15))
    pair_scale = jnp.exp(jax.random.uniform(third, (N, N, 1), minval=-1.15, maxval=1.15))
    base = jax.random.normal(first, (N, N, C))
    return jnp.clip(base * channel_scale * pair_scale, -40.0, 40.0).astype(jnp.bfloat16)


def levels(stream_key, dims, pieces, low, high):
    gain = 1.0
    for axis_at, shards_of in pieces:
        steps = jax.random.uniform(jax.random.fold_in(jax.random.fold_in(stream_key, 6), axis_at), (shards_of,), jnp.float32, low / len(pieces), high / len(pieces))
        gain = gain * jnp.repeat(jnp.exp(steps), dims[axis_at] // shards_of).reshape((-1,) + (1,) * (len(dims) - 1 - axis_at))
    return gain


def centred(key, extent, scale, most, shards=(), kind=jnp.bfloat16):
    drawn = scale * jax.random.normal(key, extent, jnp.float32)
    if shards:
        drawn = drawn * levels(key, extent, shards, -0.22, 0.18)
    return jnp.clip(drawn, -most, most).astype(kind)


def setup_inputs(seed: int = 0, part: int = 0) -> dict:
    keys = jax.random.split(jax.random.key(seed), 7)
    own_keys = jax.random.split(jax.random.fold_in(keys[6], part), 7)
    pair_input = draw_pair_input(jax.random.fold_in(jax.random.fold_in(keys[6], part), 71), part)
    gain_in = jnp.clip(1.0 + 0.1 * jax.random.normal(keys[1], (C,), jnp.float32), 0.5, 1.5)
    w_in = centred(keys[2], (C, 5 * C), C ** -0.5, 0.5)
    w_out = centred(keys[3], (C, C), C ** -0.5, 0.5)
    product_gain = jnp.clip(1.0 + 0.1 * jax.random.normal(keys[4], (C,), jnp.float32), 0.5, 1.5)
    cotangent = centred(own_keys[5], (N, N, C), 1.0, 6.0, ((0, 128),))
    return {"pair_input": pair_input, "gain_in": gain_in, "w_in": w_in, "w_out": w_out, "product_gain": product_gain, "cotangent": cotangent}


EPS = 1e-05

def layer_norm_moments(value, reduce_axis):
    vf = value.astype(jnp.float32)
    center = vf - lax.optimization_barrier(jnp.mean(vf, axis=reduce_axis, keepdims=True))
    inverse = lax.rsqrt(lax.optimization_barrier(jnp.mean(center * center, axis=reduce_axis, keepdims=True)) + EPS)
    return (center * inverse, inverse)

def layer_norm_backward(upstream, normal, inverse, reduce_axis):
    first = lax.optimization_barrier(jnp.mean(upstream, axis=reduce_axis, keepdims=True))
    second = lax.optimization_barrier(jnp.mean(upstream * normal, axis=reduce_axis, keepdims=True))
    return inverse * (upstream - first - normal * second)

def reference(pair_input, gain_in, w_in, w_out, product_gain, cotangent):
    bfloat_cast = jnp.bfloat16
    fl = jnp.float32
    width = pair_input.shape[2]
    length = pair_input.shape[1]
    zhat, zinv = layer_norm_moments(pair_input, 2)
    normed = (zhat * gain_in).astype(bfloat_cast)
    proj = jnp.einsum('ikd,de->ike', normed.astype(fl), w_in.astype(fl))
    p_left = proj[:, :, 0:width]
    g_left = jax.nn.sigmoid(proj[:, :, width:2 * width])
    p_right = proj[:, :, 2 * width:3 * width]
    g_right = jax.nn.sigmoid(proj[:, :, 3 * width:4 * width])
    gate = jax.nn.sigmoid(proj[:, :, 4 * width:])
    left = (g_left * p_left).astype(bfloat_cast)
    right = (g_right * p_right).astype(bfloat_cast)
    triangle_product = jnp.einsum('ikc,jkc->ijc', left.astype(fl), right.astype(fl)).astype(bfloat_cast)
    centered_scaled_input, inverse_deviation = layer_norm_moments(triangle_product, 2)
    input_normalized = (centered_scaled_input * product_gain).astype(bfloat_cast)
    lin = jnp.einsum('ijc,ce->ije', input_normalized.astype(fl), w_out.astype(fl))
    update = (gate * lin).astype(bfloat_cast)
    upstream = cotangent.astype(fl)
    d_lin = (upstream * gate).astype(bfloat_cast)
    d_gate = (upstream * lin * gate * (1.0 - gate)).astype(bfloat_cast)
    gw_out = jnp.einsum('ijc,ije->ce', input_normalized.astype(fl), d_lin.astype(fl))
    normed_gradient = jnp.einsum('ije,ce->ijc', d_lin.astype(fl), w_out.astype(fl))
    product_gain_gradient = lax.optimization_barrier(jnp.sum(normed_gradient * centered_scaled_input, axis=(0, 1)))
    product_gradient = layer_norm_backward(normed_gradient * product_gain, centered_scaled_input, inverse_deviation, 2).astype(bfloat_cast)
    d_left = jnp.einsum('ijc,jkc->ikc', product_gradient.astype(fl), right.astype(fl)).astype(bfloat_cast).astype(fl)
    d_right = jnp.einsum('ijc,ikc->jkc', product_gradient.astype(fl), left.astype(fl)).astype(bfloat_cast).astype(fl)
    d_factor = jnp.concatenate([d_left * g_left, d_left * p_left * g_left * (1.0 - g_left), d_right * g_right, d_right * p_right * g_right * (1.0 - g_right)], axis=2).astype(bfloat_cast)
    gw_in = jnp.concatenate([jnp.einsum('ikd,ike->de', normed.astype(fl), d_factor.astype(fl)), jnp.einsum('ikd,ike->de', normed.astype(fl), d_gate.astype(fl))], axis=1)
    d_normed = jnp.einsum('ike,de->ikd', d_factor.astype(fl), w_in[:, :4 * width].astype(fl))
    d_normed = d_normed + jnp.einsum('ike,de->ikd', d_gate.astype(fl), w_in[:, 4 * width:].astype(fl))
    gg_in = lax.optimization_barrier(jnp.sum(d_normed * zhat, axis=(0, 1)))
    grad_pair = layer_norm_backward(d_normed * gain_in, zhat, zinv, 2).astype(bfloat_cast)
    scale = 1.0 / length
    return (update, grad_pair, gw_in * scale, gw_out * scale, gg_in * scale, product_gain_gradient * scale)
```

```python
import jax
import jax.numpy as jnp
from jax import lax
from jax.sharding import PartitionSpec as P

EPS = 1e-05


def layer_norm_moments(value, reduce_axis):
    vf = value.astype(jnp.float32)
    center = vf - jnp.mean(vf, axis=reduce_axis, keepdims=True)
    inverse = lax.rsqrt(jnp.mean(center * center, axis=reduce_axis, keepdims=True) + EPS)
    return (center * inverse, inverse)


def layer_norm_backward(upstream, normal, inverse, reduce_axis):
    first = jnp.mean(upstream, axis=reduce_axis, keepdims=True)
    second = jnp.mean(upstream * normal, axis=reduce_axis, keepdims=True)
    return inverse * (upstream - first - normal * second)


def triangle(left_cols, right_cols):
    return jnp.einsum(
        "ick,jck->icj", left_cols, right_cols, preferred_element_type=jnp.float32
    ).astype(jnp.bfloat16)


def on_device(pair_input, gain_in, w_in, w_out, product_gain, cotangent):
    bfloat_cast = jnp.bfloat16
    fl = jnp.float32
    width = pair_input.shape[2]
    length = pair_input.shape[1]
    zhat, zinv = layer_norm_moments(pair_input, 2)
    normed = (zhat * gain_in).astype(bfloat_cast)
    factor_proj = jnp.einsum("rkd,de->rek", normed, w_in[:, : 4 * width], preferred_element_type=fl)
    gate_proj = jnp.einsum("rkd,de->rke", normed, w_in[:, 4 * width :], preferred_element_type=fl)
    p_left = factor_proj[:, 0:width]
    g_left = jax.nn.sigmoid(factor_proj[:, width : 2 * width])
    left_rows = (g_left * p_left).astype(bfloat_cast)
    p_right = factor_proj[:, 2 * width : 3 * width]
    g_right = jax.nn.sigmoid(factor_proj[:, 3 * width :])
    right_rows = (g_right * p_right).astype(bfloat_cast)
    left_cols, right_cols = (
        lax.all_to_all(left_rows, "res", split_axis=1, concat_axis=0, tiled=True),
        lax.all_to_all(right_rows, "res", split_axis=1, concat_axis=0, tiled=True),
    )
    prod_cols = triangle(left_cols, right_cols)
    triangle_product_rows = lax.all_to_all(
        prod_cols, "res", split_axis=0, concat_axis=1, tiled=True
    )
    centered_scaled_input, inverse_deviation = layer_norm_moments(triangle_product_rows, 1)
    input_normalized = (centered_scaled_input * product_gain[None, :, None]).astype(bfloat_cast)
    lin = jnp.einsum("rcj,ce->rje", input_normalized, w_out, preferred_element_type=fl)
    gate = jax.nn.sigmoid(gate_proj)
    update = (gate * lin).astype(bfloat_cast)
    upstream = cotangent.astype(fl)
    d_lin = (upstream * gate).astype(bfloat_cast)
    d_gate = (upstream * lin * gate * (1.0 - gate)).astype(bfloat_cast)
    gw_out = jnp.einsum("rcj,rje->ce", input_normalized, d_lin, preferred_element_type=fl)
    normed_gradient = jnp.einsum("rje,ce->rcj", d_lin, w_out, preferred_element_type=fl)
    product_gain_gradient = jnp.sum(normed_gradient * centered_scaled_input, axis=(0, 2))
    product_gradient = layer_norm_backward(
        normed_gradient * product_gain[None, :, None], centered_scaled_input, inverse_deviation, 1
    ).astype(bfloat_cast)
    d_prod_cols = lax.all_to_all(product_gradient, "res", split_axis=1, concat_axis=0, tiled=True)
    d_left_cols = jnp.einsum(
        "icj,jck->ick", d_prod_cols, right_cols, preferred_element_type=fl
    ).astype(bfloat_cast)
    d_right_cols = jnp.einsum(
        "icj,ick->jck", d_prod_cols, left_cols, preferred_element_type=fl
    ).astype(bfloat_cast)
    d_left, d_right = (
        lax.all_to_all(d_left_cols, "res", split_axis=0, concat_axis=1, tiled=True),
        lax.all_to_all(d_right_cols, "res", split_axis=0, concat_axis=1, tiled=True),
    )
    d_left = d_left.astype(fl)
    d_right = d_right.astype(fl)
    d_factor = jnp.concatenate(
        [
            d_left * g_left,
            d_left * p_left * g_left * (1.0 - g_left),
            d_right * g_right,
            d_right * p_right * g_right * (1.0 - g_right),
        ],
        axis=1,
    ).astype(bfloat_cast)
    gw_in = jnp.concatenate(
        [
            jnp.einsum("rkd,rek->de", normed, d_factor, preferred_element_type=fl),
            jnp.einsum("rkd,rke->de", normed, d_gate, preferred_element_type=fl),
        ],
        axis=1,
    )
    d_normed = jnp.einsum("rek,de->rkd", d_factor, w_in[:, : 4 * width], preferred_element_type=fl)
    d_normed = d_normed + jnp.einsum(
        "rke,de->rkd", d_gate, w_in[:, 4 * width :], preferred_element_type=fl
    )
    gg_in = jnp.sum(d_normed * zhat, axis=(0, 1))
    grad_pair = layer_norm_backward(d_normed * gain_in, zhat, zinv, 2).astype(bfloat_cast)
    parts = lax.axis_size("res")
    flat = jnp.concatenate(
        [gw_in.reshape(-1), gw_out.reshape(-1), gg_in, product_gain_gradient]
    ).reshape(parts, -1)
    pieces = lax.all_to_all(flat, "res", split_axis=0, concat_axis=0, tiled=True)
    mine = jnp.sum(pieces, axis=0, keepdims=True)
    copies = jnp.broadcast_to(mine, flat.shape)
    total = lax.all_to_all(copies, "res", split_axis=0, concat_axis=0, tiled=True).reshape(-1)
    n_in, n_out = gw_in.size, gw_out.size
    total_in = total[:n_in].reshape(gw_in.shape)
    total_out = total[n_in : n_in + n_out].reshape(gw_out.shape)
    total_gain_in = total[n_in + n_out : n_in + n_out + width]
    total_gain_out = total[n_in + n_out + width :]
    scale = 1.0 / length
    return (
        update,
        grad_pair,
        total_in * scale,
        total_out * scale,
        total_gain_in * scale,
        total_gain_out * scale,
    )


def solution(mesh):
    return jax.shard_map(
        on_device,
        mesh=mesh,
        in_specs=(
            P(("crop", "res"), None, None),
            P(),
            P(),
            P(),
            P(),
            P(("crop", "res"), None, None),
        ),
        out_specs=(
            P(("crop", "res"), None, None),
            P(("crop", "res"), None, None),
            P("crop", None),
            P("crop", None),
            P("crop"),
            P("crop"),
        ),
        check_vma=False,
    )
```

```python
import functools

import jax
import jax.numpy as jnp
from jax import lax
from jax.experimental import pallas as pl
from jax.experimental.pallas import tpu as pltpu
from jax.sharding import PartitionSpec as P

EPS = 1e-05
FL = jnp.float32
BF = jnp.bfloat16
C = 128
PIECE = 32
GROWS = 16


def dot(a, b, dims=((1,), (0,))):
    return lax.dot_general(a, b, (dims, ((), ())), preferred_element_type=FL)


NT = ((1,), (1,))
TN = ((0,), (0,))


def sigmoid(x):
    return jax.nn.sigmoid(x)


def kernel(
    parts, rows, length,
    z_ref, gain_in_ref, w_in_ref, w_out_ref, gain_out_ref, cot_ref,
    upd_ref, gp_ref, gwi_ref, gwo_ref, gains_ref,
    send, recv, gsend, grecv, bsend, brecv, packed, opened, natural,
    left_m, right_m, dprod_m,
    zhat, zinv, normed, p_l, s_l, p_r, s_r, s_g, cot_t, upd_t, xn, d_lin, d_proj,
    w_in_t, w_out_t, gain_in_c, gain_out_c, grads,
    send_sem, recv_sem, gsend_sem, grecv_sem, bsend_sem, brecv_sem,
):
    tiles = length // C
    owners = gsend.shape[0]
    me = lax.axis_index("res")

    barrier = pltpu.get_barrier_semaphore()

    def peer(step):
        return lax.rem(me + lax.rem(step * 37, parts), parts)

    def greet(step, carry):
        pl.semaphore_signal(
            barrier, inc=1, device_id={"res": peer(step)}, device_id_type=pl.DeviceIdType.MESH
        )
        return carry

    lax.fori_loop(1, parts, greet, 0)

    def copy_to(stage, to):
        return pltpu.make_async_remote_copy(
            src_ref=send.at[stage, to],
            dst_ref=recv.at[stage, me],
            send_sem=send_sem.at[stage],
            recv_sem=recv_sem.at[stage],
            device_id={"res": to},
            device_id_type=pl.DeviceIdType.MESH,
        )

    def all_pieces(stage):
        return pltpu.make_async_remote_copy(
            src_ref=send.at[stage, pl.ds(0, parts - 1)],
            dst_ref=recv.at[stage, pl.ds(0, parts - 1)],
            send_sem=send_sem.at[stage],
            recv_sem=recv_sem.at[stage],
            device_id={"res": peer(1)},
            device_id_type=pl.DeviceIdType.MESH,
        )

    def slab(row, tile):
        return pl.ds(row * tiles + tile, parts, stride=PIECE)

    def pack(row, value):
        for tile in range(tiles):
            packed[slab(row, tile), :] = value[:, tile * C : (tile + 1) * C]

    def unpack(row):
        return jnp.concatenate([opened[slab(row, tile), :] for tile in range(tiles)], axis=1)

    def send_packed(stage):
        send[stage] = packed[...].astype(BF).reshape(parts, PIECE, C)

        def start(step, carry):
            copy_to(stage, peer(step)).start()
            return carry

        lax.fori_loop(1, parts, start, 0)
        recv[stage, me] = send[stage, me]

    def receive(stage):
        all_pieces(stage).wait_recv()
        opened[...] = recv[stage].reshape(parts * PIECE, C).astype(FL)

    def square(value):
        return jnp.transpose(value.astype(FL))

    eye = (
        lax.broadcasted_iota(jnp.int32, (C, C), 0) == lax.broadcasted_iota(jnp.int32, (C, C), 1)
    ).astype(BF)
    for block in range(5):
        w_in_t[block * C : (block + 1) * C, :] = square(
            w_in_ref[:, block * C : (block + 1) * C]
        ).astype(BF)
    w_out_t[...] = square(w_out_ref[...]).astype(BF)
    gain_in_c[...] = square(jnp.broadcast_to(gain_in_ref[...], (C, C)))
    gain_out_c[...] = square(jnp.broadcast_to(gain_out_ref[...], (C, C)))
    packed[...] = jnp.zeros(packed.shape, FL)

    for row in range(rows):
        zt = dot(eye, z_ref[row], NT)
        center = zt - jnp.mean(zt, axis=0, keepdims=True)
        inverse = lax.rsqrt(jnp.mean(center * center, axis=0, keepdims=True) + EPS)
        zh = center * inverse
        zhat[row] = zh
        zinv[row] = inverse
        normed[row] = (zh * gain_in_c[:, :1]).astype(BF)
        proj = dot(w_in_t[: 2 * C, :], normed[row])
        s_l[row] = sigmoid(proj[C:])
        p_l[row] = proj[:C]
        pack(row, p_l[row] * s_l[row])
    pl.semaphore_wait(barrier, parts - 1)
    send_packed(0)
    for row in range(rows):
        proj = dot(w_in_t[2 * C : 4 * C, :], normed[row])
        s_r[row] = sigmoid(proj[C:])
        p_r[row] = proj[:C]
        pack(row, p_r[row] * s_r[row])
    send_packed(1)
    for row in range(rows):
        s_g[row] = sigmoid(dot(w_in_t[4 * C :, :], normed[row]))
        cot_t[row] = dot(eye, cot_ref[row], NT)

    receive(0)
    for row in range(rows):
        left_m[row * parts : (row + 1) * parts, :] = unpack(row).astype(BF)
    receive(1)
    for tile in range(tiles):
        for row in range(rows):
            natural[tile, pl.ds(row, parts, stride=rows), :] = opened[slab(row, tile), :]
        right_m[:, tile * C : (tile + 1) * C] = natural[tile].astype(BF)
    for row in range(rows):
        pack(row, dot(left_m[row * parts : (row + 1) * parts, :], right_m[...], NT))
    send_packed(2)

    receive(2)
    gg_out = jnp.zeros((C, C), FL)
    for row in range(rows):
        prod = unpack(row)
        center = prod - jnp.mean(prod, axis=0, keepdims=True)
        inverse = lax.rsqrt(jnp.mean(center * center, axis=0, keepdims=True) + EPS)
        xh = center * inverse
        xn[row] = (xh * gain_out_c[:, :1]).astype(BF)
        lin = dot(w_out_t[...], xn[row])
        s = s_g[row]
        upd_t[row] = s * lin
        g = cot_t[row]
        d_lin[row] = (g * s).astype(BF)
        d_proj[row, 4 * C :, :] = (g * lin * s * (1.0 - s)).astype(BF)
        d_xn = dot(w_out_ref[...], d_lin[row])
        both = d_xn * xh
        for tile in range(tiles):
            gg_out = gg_out + both[:, tile * C : (tile + 1) * C]
        h = d_xn * gain_out_c[:, :1]
        first = jnp.mean(h, axis=0, keepdims=True)
        second = jnp.mean(h * xh, axis=0, keepdims=True)
        pack(row, inverse * (h - first - xh * second))
    send_packed(3)
    for row in range(rows):
        for tile in range(tiles):
            upd_ref[row, tile * C : (tile + 1) * C, :] = jnp.transpose(
                upd_t[row, :, tile * C : (tile + 1) * C]
            ).astype(BF)
    gw = jnp.zeros((C, C), FL)
    gw_gate = jnp.zeros((C, C), FL)
    for row in range(rows):
        gw = gw + dot(xn[row], d_lin[row], NT)
        gw_gate = gw_gate + dot(normed[row], d_proj[row, 4 * C :, :], NT)
    grads[4 * C : 5 * C, :] = gw_gate
    grads[5 * C : 6 * C, :] = gw
    grads[6 * C :, :] = jnp.zeros((GROWS, C), FL)
    grads[6 * C + 1 : 6 * C + 2, :] = jnp.sum(jnp.transpose(gg_out), axis=0, keepdims=True)

    receive(3)
    for row in range(rows):
        dprod_m[row * parts : (row + 1) * parts, :] = unpack(row).astype(BF)
    for row in range(rows):
        pack(row, dot(dprod_m[row * parts : (row + 1) * parts, :], right_m[...]))
    send_packed(4)
    for tile in range(tiles):
        part = dot(dprod_m[:, tile * C : (tile + 1) * C], left_m[...], TN)
        for across in range(tiles):
            natural[across, tile * C : (tile + 1) * C, :] = part[:, across * C : (across + 1) * C]
    for row in range(rows):
        for tile in range(tiles):
            packed[slab(row, tile), :] = natural[tile, pl.ds(row, parts, stride=rows), :]
    send_packed(5)

    for side, p_ref, s_ref in ((0, p_l, s_l), (1, p_r, s_r)):
        receive(4 + side)
        base = side * 2 * C
        total = jnp.zeros((C, 2 * C), FL)
        for row in range(rows):
            d = unpack(row)
            s = s_ref[row]
            d_proj[row, base : base + C, :] = (d * s).astype(BF)
            d_proj[row, base + C : base + 2 * C, :] = (d * p_ref[row] * s * (1.0 - s)).astype(BF)
            total = total + dot(normed[row], d_proj[row, base : base + 2 * C, :], NT)
        grads[base : base + C, :] = total[:, :C]
        grads[base + C : base + 2 * C, :] = total[:, C:]

    gg_in = jnp.zeros((C, C), FL)
    for row in range(rows):
        d_normed = dot(w_in_ref[...], d_proj[row])
        p_l[row] = d_normed
        both = d_normed * zhat[row]
        for tile in range(tiles):
            gg_in = gg_in + both[:, tile * C : (tile + 1) * C]
    grads[6 * C : 6 * C + 1, :] = jnp.sum(jnp.transpose(gg_in), axis=0, keepdims=True)
    gsend[...] = grads[...].astype(BF).reshape(owners, GROWS, C)

    chip = lax.div(me, 2)
    own = jnp.logical_and(lax.rem(me, 2) == 0, chip < owners)

    def gcopy(q):
        return pltpu.make_async_remote_copy(
            src_ref=gsend.at[q],
            dst_ref=grecv.at[me],
            send_sem=gsend_sem,
            recv_sem=grecv_sem,
            device_id={"res": 2 * q},
            device_id_type=pl.DeviceIdType.MESH,
        )

    def gstart(step, carry):
        q = lax.rem(chip + step, owners)

        @pl.when(2 * q != me)
        def _():
            gcopy(q).start()

        return carry

    lax.fori_loop(0, owners, gstart, 0)

    @pl.when(own)
    def _():
        grecv[me] = gsend[chip]

    for row in range(rows):
        zh = zhat[row]
        h = p_l[row] * gain_in_c[:, :1]
        first = jnp.mean(h, axis=0, keepdims=True)
        second = jnp.mean(h * zh, axis=0, keepdims=True)
        out = zinv[row] * (h - first - zh * second)
        for tile in range(tiles):
            gp_ref[row, tile * C : (tile + 1) * C, :] = jnp.transpose(
                out[:, tile * C : (tile + 1) * C]
            ).astype(BF)

    def gall(dst, recv_on, count, src, send_on):
        return pltpu.make_async_remote_copy(
            src_ref=src.at[pl.ds(0, count)],
            dst_ref=dst.at[pl.ds(0, count)],
            send_sem=send_on,
            recv_sem=recv_on,
            device_id={"res": peer(1)},
            device_id_type=pl.DeviceIdType.MESH,
        )

    @pl.when(own)
    def _():
        gall(grecv, grecv_sem, parts - 1, grecv, gsend_sem).wait_recv()
        total = jnp.sum(grecv[...].astype(FL), axis=0)
        bsend[...] = (total * (1.0 / length)).astype(BF)

        def bstart(step, carry):
            pltpu.make_async_remote_copy(
                src_ref=bsend,
                dst_ref=brecv.at[chip],
                send_sem=bsend_sem,
                recv_sem=brecv_sem,
                device_id={"res": peer(step)},
                device_id_type=pl.DeviceIdType.MESH,
            ).start()
            return carry

        lax.fori_loop(1, parts, bstart, 0)
        brecv[chip] = bsend[...]
        gall(brecv, brecv_sem, owners - 1, brecv, bsend_sem).wait_recv()
        gall(gsend, gsend_sem, owners - 1, gsend, gsend_sem).wait_send()
        gall(grecv, grecv_sem, parts - 1, grecv, bsend_sem).wait_send()

    @pl.when(jnp.logical_not(own))
    def _():
        gall(brecv, brecv_sem, owners, brecv, bsend_sem).wait_recv()
        gall(gsend, gsend_sem, owners, gsend, gsend_sem).wait_send()

    total = brecv[...].astype(FL).reshape(owners * GROWS, C)
    for block in range(5):
        gwi_ref[:, block * C : (block + 1) * C] = total[block * C : (block + 1) * C]
    gwo_ref[...] = total[5 * C : 6 * C]
    gains_ref[...] = total[6 * C : 6 * C + 8]
    for stage in range(6):
        all_pieces(stage).wait_send()


def on_device(pair_input, gain_in, w_in, w_out, product_gain, cotangent):
    rows, length, width = pair_input.shape
    parts = lax.axis_size("res")
    owners = (6 * C) // GROWS + 1
    held = (rows, C, length)
    vmem = pl.BlockSpec(memory_space=pltpu.VMEM)
    sem = pltpu.SemaphoreType.DMA
    upd, gp, gwi, gwo, gains = pl.pallas_call(
        functools.partial(kernel, parts, rows, length),
        out_shape=(
            jax.ShapeDtypeStruct(pair_input.shape, BF),
            jax.ShapeDtypeStruct(pair_input.shape, BF),
            jax.ShapeDtypeStruct(w_in.shape, FL),
            jax.ShapeDtypeStruct(w_out.shape, FL),
            jax.ShapeDtypeStruct((8, C), FL),
        ),
        in_specs=[vmem] * 6,
        out_specs=[vmem] * 5,
        scratch_shapes=[
            pltpu.VMEM((6, parts, PIECE, C), BF),
            pltpu.VMEM((6, parts, PIECE, C), BF),
            pltpu.VMEM((owners, GROWS, C), BF),
            pltpu.VMEM((parts, GROWS, C), BF),
            pltpu.VMEM((GROWS, C), BF),
            pltpu.VMEM((owners, GROWS, C), BF),
            pltpu.VMEM((parts * PIECE, C), FL),
            pltpu.VMEM((parts * PIECE, C), FL),
            pltpu.VMEM((length // C, length, C), FL),
            pltpu.VMEM((length, length), BF),
            pltpu.VMEM((length, length), BF),
            pltpu.VMEM((length, length), BF),
            pltpu.VMEM(held, FL),
            pltpu.VMEM((rows, 1, length), FL),
            pltpu.VMEM(held, BF),
            pltpu.VMEM(held, FL),
            pltpu.VMEM(held, FL),
            pltpu.VMEM(held, FL),
            pltpu.VMEM(held, FL),
            pltpu.VMEM(held, FL),
            pltpu.VMEM(held, FL),
            pltpu.VMEM(held, FL),
            pltpu.VMEM(held, BF),
            pltpu.VMEM(held, BF),
            pltpu.VMEM((rows, 5 * C, length), BF),
            pltpu.VMEM((5 * C, C), BF),
            pltpu.VMEM((C, C), BF),
            pltpu.VMEM((C, C), FL),
            pltpu.VMEM((C, C), FL),
            pltpu.VMEM((owners * GROWS, C), FL),
            sem((6,)),
            sem((6,)),
            sem,
            sem,
            sem,
            sem,
        ],
        compiler_params=pltpu.CompilerParams(
            collective_id=0, has_side_effects=True, vmem_limit_bytes=58 * 2**20
        ),
    )(pair_input, gain_in.reshape(1, C), w_in, w_out, product_gain.reshape(1, C), cotangent)
    return upd, gp, gwi, gwo, gains[0], gains[1]


def solution(mesh):
    return jax.shard_map(
        on_device,
        mesh=mesh,
        in_specs=(
            P(("crop", "res"), None, None),
            P(),
            P(),
            P(),
            P(),
            P(("crop", "res"), None, None),
        ),
        out_specs=(
            P(("crop", "res"), None, None),
            P(("crop", "res"), None, None),
            P("crop", None),
            P("crop", None),
            P("crop"),
            P("crop"),
        ),
        check_vma=False,
    )
```

```python
import functools

import jax
import jax.numpy as jnp
from jax import lax
from jax.experimental import pallas as pl
from jax.experimental.pallas import tpu as pltpu
from jax.sharding import PartitionSpec as P

EPS = 1e-05
FL = jnp.float32
BF = jnp.bfloat16
C = 128
LINE = 8
GROUP = 2 * LINE
GROWS = 16
SIDE = 7
ROUND = (1, 7, 2, 6, 3, 5, 4)
CHUNKS = ((0, 2), (2, 3))


def dot(a, b, dims=((1,), (0,))):
    return lax.dot_general(a, b, (dims, ((), ())), preferred_element_type=FL)


NT = ((1,), (1,))


def padded(count, tiles):
    return -(-(LINE * count * tiles) // 16) * 16


def sigmoid(x):
    return jax.nn.sigmoid(x)


def kernel(
    rows, length,
    z_ref, gain_in_ref, w_in_ref, w_out_ref, gain_out_ref, cot_ref,
    upd_ref, gp_ref, gwi_ref, gwo_ref, gains_ref,
    send1, recv1, send2, recv2, mixed,
    g_send, g_recv, h_send, h_recv, o_send, c_recv, d_recv,
    left_m, right_m, dprod_m, turned_m, order, order_t, wide,
    zhat, zinv, normed, p_l, s_l, p_r, s_r, s_g, cot_t, upd_t, xn, d_lin, d_proj,
    w_in_t, w_in_p, w_out_t, w_out_p, gain_in_c, gain_out_c, perm, grads,
    send_sem1, recv_sem1, send_sem2, recv_sem2, g_sems,
):
    tiles = length // C

    def sizes(chunk):
        first, count = CHUNKS[chunk]
        start = 0 if chunk == 0 else padded(CHUNKS[0][1], tiles)
        base = 0 if chunk == 0 else LINE * GROUP * CHUNKS[0][1]
        return first, count, start, padded(count, tiles), LINE * count, base

    me = lax.axis_index("res")
    z = me // GROUP
    y = (me // 2) % LINE
    core = me % 2
    a = y + core * (z - y)
    b = z + core * (y - z)
    step_a = 2 + (GROUP - 2) * core
    step_b = GROUP - (GROUP - 2) * core

    def device(at_a, at_b, at_core):
        return at_a * step_a + at_b * step_b + at_core

    def remote(src, dst, on_send, on_recv, to):
        return pltpu.make_async_remote_copy(
            src_ref=src,
            dst_ref=dst,
            send_sem=on_send,
            recv_sem=on_recv,
            device_id={"res": to},
            device_id_type=pl.DeviceIdType.MESH,
        )

    other = device(a, b, 1 - core)
    barrier = pltpu.get_barrier_semaphore()

    def greet(to):
        pl.semaphore_signal(
            barrier, inc=1, device_id={"res": to}, device_id_type=pl.DeviceIdType.MESH
        )

    greet(other)
    for t in ROUND:
        for at_core in (0, 1):
            greet(device((a + t) % LINE, b, at_core))
            greet(device(a, (b + t) % LINE, at_core))

    def send_rows(stage, chunk):
        first, count = CHUNKS[chunk]
        part = pl.ds(first, count)
        for t in ROUND:
            at_a = (a + t) % LINE
            remote(
                send1.at[stage, at_a, part],
                recv1.at[stage, a, part],
                send_sem1.at[stage, chunk],
                recv_sem1.at[stage, chunk],
                device(at_a, b, core),
            ).start()
        recv1[stage, a, part] = send1[stage, a, part]

    def all_a(stage, chunk):
        first, count = CHUNKS[chunk]
        return remote(
            send1.at[stage, pl.ds(0, LINE - 1), pl.ds(first, count)],
            recv1.at[stage, pl.ds(0, LINE - 1), pl.ds(first, count)],
            send_sem1.at[stage, chunk],
            recv_sem1.at[stage, chunk],
            other,
        )

    def all_b(stage, chunk):
        _, _, start, piece, _, _ = sizes(chunk)
        return remote(
            send2.at[stage, pl.ds(0, GROUP - 1), pl.ds(start, piece)],
            recv2.at[stage, pl.ds(0, GROUP - 1), pl.ds(start, piece)],
            send_sem2.at[stage, chunk],
            recv_sem2.at[stage, chunk],
            other,
        )

    def place(stage, row, value):
        value = value.astype(BF)
        for at in range(LINE):
            send1[stage, at, row] = value[at * GROUP : (at + 1) * GROUP]

    def relay_rows(stage, chunk):
        first, count, start, piece, _, _ = sizes(chunk)
        part = pl.ds(start, piece)
        stride = piece + 1
        all_a(stage, chunk).wait_recv()
        for at in range(LINE):
            for row in range(count):
                block = recv1[stage, at, first + row].astype(FL)
                for tile in range(tiles):
                    where = (at * count + row) * tiles + tile
                    mixed[pl.ds(where, GROUP, stride=stride), :] = block[
                        :, tile * C : (tile + 1) * C
                    ]
        for q in range(GROUP):
            send2[stage, q, part] = mixed[q * stride : q * stride + piece, :].astype(BF)
        mine = b * 2 + core
        for t in (0,) + ROUND:
            at_b = (b + t) % LINE
            for turn in (0, 1):
                if t == 0 and turn == 0:
                    continue
                at_core = (core + turn) % 2
                remote(
                    send2.at[stage, at_b * 2 + at_core, part],
                    recv2.at[stage, mine, part],
                    send_sem2.at[stage, chunk],
                    recv_sem2.at[stage, chunk],
                    device(a, at_b, at_core),
                ).start()
        recv2[stage, mine, part] = send2[stage, mine, part]

    def take_channel(stage, chunk, into):
        first, count, start, piece, lot, base = sizes(chunk)
        all_b(stage, chunk).wait_recv()
        for slot in range(GROUP):
            mixed[slot * piece : (slot + 1) * piece, :] = recv2[
                stage, slot, start : start + piece
            ].astype(FL)
        for at in range(LINE):
            top = base + at * 2 * lot
            for tile in range(tiles):
                both = [
                    mixed[pl.ds((at * 2 + k) * piece + tile, lot, stride=tiles), :]
                    for k in (0, 1)
                ]
                into[top : top + 2 * lot, tile * C : (tile + 1) * C] = (
                    jnp.concatenate(both, axis=0).astype(BF)
                )

    def of(factor, chunk):
        _, _, _, _, lot, base = sizes(chunk)
        return factor[base : base + GROUP * lot, :]

    def send_channel(stage, chunk, whole):
        _, _, start, piece, lot, _ = sizes(chunk)
        slab = pl.ds(start, piece)
        wide[: GROUP * lot, :] = whole
        for t in (0,) + ROUND:
            at_b = (b + t) % LINE
            part = wide[pl.ds(pl.multiple_of(at_b * 2 * lot, GROUP), 2 * lot), :]
            for k in (0, 1):
                for tile in range(tiles):
                    mixed[pl.ds(k * piece + tile, lot, stride=tiles), :] = part[
                        k * lot : (k + 1) * lot, tile * C : (tile + 1) * C
                    ]
            for k in (0, 1):
                send2[stage, at_b * 2 + k, slab] = mixed[k * piece : (k + 1) * piece, :].astype(BF)
                to = (at_b * GROUP + y * 2) if k == 0 else (z * GROUP + at_b * 2 + 1)
                copy = remote(
                    send2.at[stage, at_b * 2 + k, slab],
                    recv2.at[stage, (z if k == 0 else y) * 2 + core, slab],
                    send_sem2.at[stage, chunk],
                    recv_sem2.at[stage, chunk],
                    to,
                )
                if t == 0:

                    @pl.when(core == k)
                    def _():
                        recv2[stage, at_b * 2 + k, slab] = send2[stage, at_b * 2 + k, slab]

                    @pl.when(core != k)
                    def _():
                        copy.start()

                else:
                    copy.start()

    def relay_channel(stage, chunk):
        first, count, start, piece, _, _ = sizes(chunk)
        stride = piece + 1
        all_b(stage, chunk).wait_recv()
        for q in range(GROUP):
            mixed[q * stride : q * stride + piece, :] = recv2[
                stage, q, start : start + piece
            ].astype(FL)
        for at in range(LINE):
            for row in range(count):
                for tile in range(tiles):
                    where = (at * count + row) * tiles + tile
                    send1[stage, at, first + row, :, tile * C : (tile + 1) * C] = mixed[
                        pl.ds(where, GROUP, stride=stride), :
                    ].astype(BF)
        send_rows(stage, chunk)

    def take_row(stage, row):
        return jnp.concatenate([recv1[stage, at, row] for at in range(LINE)], axis=0).astype(FL)

    def chunk_rows(chunk):
        first, count = CHUNKS[chunk]
        return range(first, first + count)

    def iota(shape, dim):
        return lax.broadcasted_iota(jnp.int32, shape, dim)

    eye = (iota((C, C), 0) == iota((C, C), 1)).astype(BF)
    q = iota((C, C), 0)
    home = (q >> 4) * step_a + ((q >> 1) & 7) * step_b + (q & 1)
    perm_f = (home == iota((C, C), 1)).astype(FL)
    perm[...] = perm_f.astype(BF)
    for block in range(5):
        sort = perm[...] if block < 4 else eye
        cols = slice(block * C, (block + 1) * C)
        w_in_t[cols, :] = dot(sort, w_in_ref[:, cols], NT).astype(BF)
        w_in_p[:, cols] = dot(w_in_ref[:, cols], sort, NT).astype(BF)
    w_out_p[...] = dot(perm[...], w_out_ref[...]).astype(BF)
    w_out_t[...] = jnp.transpose(dot(perm[...], w_out_ref[...])).astype(BF)
    gain_in_c[...] = jnp.transpose(jnp.broadcast_to(gain_in_ref[...], (C, C)))
    gain_out_c[...] = jnp.broadcast_to(
        jnp.sum(perm_f * gain_out_ref[...], axis=1, keepdims=True), (C, C)
    )
    mixed[...] = jnp.zeros(mixed.shape, FL)

    for chunk in (0, 1):
        for row in chunk_rows(chunk):
            zt = dot(eye, z_ref[row], NT)
            center = zt - jnp.mean(zt, axis=0, keepdims=True)
            inverse = lax.rsqrt(jnp.mean(center * center, axis=0, keepdims=True) + EPS)
            zh = center * inverse
            zhat[row] = zh
            zinv[row] = inverse
            normed[row] = (zh * gain_in_c[:, :1]).astype(BF)
            proj = dot(w_in_t[: 2 * C, :], normed[row])
            s_l[row] = sigmoid(proj[C:])
            p_l[row] = proj[:C]
            place(0, row, p_l[row] * s_l[row])
        if chunk == 0:
            pl.semaphore_wait(barrier, 4 * LINE - 3)
        send_rows(0, chunk)
    for chunk in (0, 1):
        for row in chunk_rows(chunk):
            proj = dot(w_in_t[2 * C : 4 * C, :], normed[row])
            s_r[row] = sigmoid(proj[C:])
            p_r[row] = proj[:C]
            place(1, row, p_r[row] * s_r[row])
        send_rows(1, chunk)
    relay_rows(0, 0)
    relay_rows(0, 1)
    for row in range(rows):
        s_g[row] = sigmoid(dot(w_in_t[4 * C :, :], normed[row]))
    relay_rows(1, 0)
    relay_rows(1, 1)
    for row in range(rows):
        cot_t[row] = dot(eye, cot_ref[row], NT)

    def natural(p):
        split = LINE * GROUP * CHUNKS[0][1]
        second = p >= split
        count = jnp.where(second, float(CHUNKS[1][1]), float(CHUNKS[0][1]))
        pf = p.astype(FL) + 0.5 - jnp.where(second, float(split), 0.0)
        at_b = jnp.floor(pf / (count * GROUP))
        pf = pf - at_b * (count * GROUP)
        at_core = jnp.floor(pf / (count * LINE))
        pf = pf - at_core * (count * LINE)
        at_a = jnp.floor(pf / count)
        row = pf - 0.5 - at_a * count + jnp.where(second, float(CHUNKS[1][0]), 0.0)
        at_z = at_b + at_core * (at_a - at_b)
        at_y = at_a + at_core * (at_b - at_a)
        return ((at_z * GROUP + at_y * 2 + at_core) * rows + row + 0.5).astype(jnp.int32)

    order[...] = (iota((length, length), 0) == natural(iota((1, length), 1))).astype(FL).astype(BF)
    order_t[...] = (
        (iota((length, length), 1) == natural(iota((length, 1), 0))).astype(FL).astype(BF)
    )

    take_channel(0, 0, left_m)
    take_channel(0, 1, left_m)
    take_channel(1, 0, turned_m)
    take_channel(1, 1, turned_m)
    right_m[...] = dot(order[...], turned_m[...]).astype(BF)
    for chunk in (0, 1):
        send_channel(2, chunk, dot(of(left_m, chunk), right_m[...], NT))
    for chunk in (0, 1):
        relay_channel(2, chunk)

    gg_out = jnp.zeros((C, C), FL)
    for chunk in (0, 1):
        all_a(2, chunk).wait_recv()
        for row in chunk_rows(chunk):
            prod = take_row(2, row)
            center = prod - jnp.mean(prod, axis=0, keepdims=True)
            inverse = lax.rsqrt(jnp.mean(center * center, axis=0, keepdims=True) + EPS)
            xh = center * inverse
            xn[row] = (xh * gain_out_c[:, :1]).astype(BF)
            lin = dot(w_out_t[...], xn[row])
            s = s_g[row]
            upd_t[row] = s * lin
            g = cot_t[row]
            d_lin[row] = (g * s).astype(BF)
            d_proj[row, 4 * C :, :] = (g * lin * s * (1.0 - s)).astype(BF)
            d_xn = dot(w_out_p[...], d_lin[row])
            both = d_xn * xh
            for tile in range(tiles):
                gg_out = gg_out + both[:, tile * C : (tile + 1) * C]
            h = d_xn * gain_out_c[:, :1]
            first = jnp.mean(h, axis=0, keepdims=True)
            second = jnp.mean(h * xh, axis=0, keepdims=True)
            place(3, row, inverse * (h - first - xh * second))
        send_rows(3, chunk)
    relay_rows(3, 0)
    relay_rows(3, 1)
    gw = jnp.zeros((C, C), FL)
    gw_gate = jnp.zeros((C, C), FL)
    for row in range(rows):
        gw = gw + dot(xn[row], d_lin[row], NT)
        gw_gate = gw_gate + dot(normed[row], d_proj[row, 4 * C :, :], NT)
    grads[4 * C : 5 * C, :] = gw_gate.astype(BF)
    grads[5 * C : 6 * C, :] = dot(perm[...], gw.astype(BF)).astype(BF)
    for row in range(rows):
        for tile in range(tiles):
            upd_ref[row, tile * C : (tile + 1) * C, :] = jnp.transpose(
                upd_t[row, :, tile * C : (tile + 1) * C]
            ).astype(BF)

    for chunk in (0, 1):
        take_channel(3, chunk, dprod_m)
        send_channel(4, chunk, dot(of(dprod_m, chunk), right_m[...]))
    turned_m[...] = dot(order_t[...], dprod_m[...], NT).astype(BF)
    for chunk in (0, 1):
        send_channel(5, chunk, dot(of(turned_m, chunk), left_m[...]))
    for stage in (4, 5):
        for chunk in (0, 1):
            relay_channel(stage, chunk)

    def write_rows(picked):
        for row in picked:
            zh = zhat[row]
            h = p_l[row] * gain_in_c[:, :1]
            first = jnp.mean(h, axis=0, keepdims=True)
            second = jnp.mean(h * zh, axis=0, keepdims=True)
            out = zinv[row] * (h - first - zh * second)
            for tile in range(tiles):
                gp_ref[row, tile * C : (tile + 1) * C, :] = jnp.transpose(
                    out[:, tile * C : (tile + 1) * C]
                ).astype(BF)

    gg_in = jnp.zeros((C, C), FL)
    for side, p_ref, s_ref in ((0, p_l, s_l), (1, p_r, s_r)):
        base = side * 2 * C
        total = jnp.zeros((C, 2 * C), FL)
        for chunk in (0, 1):
            all_a(4 + side, chunk).wait_recv()
            for row in chunk_rows(chunk):
                d = take_row(4 + side, row)
                s = s_ref[row]
                d_proj[row, base : base + C, :] = (d * s).astype(BF)
                d_proj[row, base + C : base + 2 * C, :] = (
                    d * p_ref[row] * s * (1.0 - s)
                ).astype(BF)
                total = total + dot(normed[row], d_proj[row, base : base + 2 * C, :], NT)
                if side == 1:
                    d_normed = dot(w_in_p[...], d_proj[row])
                    p_l[row] = d_normed
                    both = d_normed * zhat[row]
                    for tile in range(tiles):
                        gg_in = gg_in + both[:, tile * C : (tile + 1) * C]
            if side == 1 and chunk == 0:
                write_rows(chunk_rows(0))
        total = total.astype(BF)
        grads[base : base + C, :] = dot(total[:, :C], perm[...]).astype(BF)
        grads[base + C : base + 2 * C, :] = dot(total[:, C:], perm[...]).astype(BF)

    gg_in = jnp.sum(jnp.transpose(gg_in), axis=0, keepdims=True)
    gg_out = jnp.sum(jnp.transpose(gg_out), axis=0, keepdims=True)
    gg_out = dot(jnp.broadcast_to(gg_out, (GROWS, C)).astype(BF), perm[...])
    line = iota((GROWS, C), 0)
    grads[6 * C :, :] = jnp.where(line == 0, jnp.broadcast_to(gg_in, (GROWS, C)), gg_out).astype(BF)

    def both_ways(u, v):
        return v + core * (u - v), u + core * (v - u)

    for u in range(SIDE):
        for v in range(SIDE):
            at = (u * SIDE + v) * GROWS
            g_send[both_ways(u, v)] = grads[at : at + GROWS, :]

    in_a = a < SIDE
    in_b = b < SIDE
    owner = jnp.logical_and(in_a, in_b)
    for t in ROUND:
        at_a = (a + t) % LINE

        @pl.when(at_a < SIDE)
        def _():
            remote(
                g_send.at[at_a], g_recv.at[a], g_sems.at[0], g_sems.at[1], device(at_a, b, core)
            ).start()

    def some(ref, count, on_send, on_recv):
        return remote(ref.at[pl.ds(0, count)], ref.at[pl.ds(0, count)], on_send, on_recv, other)

    write_rows(range(2, 3))
    mine = b * 2 + core

    @pl.when(in_a)
    def _():
        g_recv[a] = g_send[a]
        some(g_recv, LINE - 1, g_sems.at[0], g_sems.at[1]).wait_recv()
        h_send[...] = jnp.sum(g_recv[...].astype(FL), axis=0).astype(BF)
        for t in (0,) + ROUND:
            at_b = (b + t) % LINE
            for turn in (0, 1):
                if t == 0 and turn == 0:
                    continue
                at_core = (core + turn) % 2

                @pl.when(at_b < SIDE)
                def _():
                    remote(
                        h_send.at[at_b],
                        h_recv.at[mine],
                        g_sems.at[2],
                        g_sems.at[3],
                        device(a, at_b, at_core),
                    ).start()

    write_rows(range(3, 4))

    @pl.when(owner)
    def _():
        h_recv[mine] = h_send[b]
        some(h_recv, GROUP - 1, g_sems.at[2], g_sems.at[3]).wait_recv()
        total = jnp.sum(h_recv[...].astype(FL), axis=0) * (1.0 / length)
        o_send[...] = total.astype(BF)
        for t in ROUND:
            remote(
                o_send, c_recv.at[b], g_sems.at[4], g_sems.at[5], device(a, (b + t) % LINE, core)
            ).start()
        c_recv[b] = o_send[...]

    write_rows(range(4, rows))

    @pl.when(in_a)
    def _():
        @pl.when(in_b)
        def _():
            some(c_recv, SIDE - 1, g_sems.at[4], g_sems.at[5]).wait_recv()

        @pl.when(jnp.logical_not(in_b))
        def _():
            some(c_recv, SIDE, g_sems.at[4], g_sems.at[5]).wait_recv()

        for t in ROUND:
            remote(
                c_recv, d_recv.at[a], g_sems.at[6], g_sems.at[7], device((a + t) % LINE, b, core)
            ).start()
        d_recv[a] = c_recv[...]
        some(d_recv, SIDE - 1, g_sems.at[6], g_sems.at[7]).wait_recv()

    @pl.when(jnp.logical_not(in_a))
    def _():
        some(d_recv, SIDE, g_sems.at[6], g_sems.at[7]).wait_recv()

    per = C // GROWS
    for u in range(SIDE):
        for v in range(SIDE):
            block, at = divmod(u * SIDE + v, per)
            value = d_recv[both_ways(u, v)].astype(FL)
            at = at * GROWS
            if block < 5:
                gwi_ref[at : at + GROWS, block * C : (block + 1) * C] = value
            elif block == 5:
                gwo_ref[at : at + GROWS, :] = value
            else:
                gains_ref[...] = value[:8]

    @pl.when(in_a)
    def _():
        some(g_send, SIDE - 1, g_sems.at[0], g_sems.at[1]).wait_send()
        some(g_recv, LINE - 1, g_sems.at[6], g_sems.at[7]).wait_send()

        @pl.when(in_b)
        def _():
            some(h_recv, GROUP - 3, g_sems.at[2], g_sems.at[3]).wait_send()
            some(h_recv, LINE - 1, g_sems.at[4], g_sems.at[5]).wait_send()

        @pl.when(jnp.logical_not(in_b))
        def _():
            some(h_recv, GROUP - 2, g_sems.at[2], g_sems.at[3]).wait_send()

    @pl.when(jnp.logical_not(in_a))
    def _():
        some(g_send, SIDE, g_sems.at[0], g_sems.at[1]).wait_send()

    for stage in range(6):
        for chunk in (0, 1):
            all_a(stage, chunk).wait_send()
            all_b(stage, chunk).wait_send()


def on_device(pair_input, gain_in, w_in, w_out, product_gain, cotangent):
    rows, length, width = pair_input.shape
    piece = sum(padded(count, length // C) for _, count in CHUNKS)
    held = (rows, C, length)
    square = (length, length)
    vmem = pl.BlockSpec(memory_space=pltpu.VMEM)
    sem = pltpu.SemaphoreType.DMA
    upd, gp, gwi, gwo, gains = pl.pallas_call(
        functools.partial(kernel, rows, length),
        out_shape=(
            jax.ShapeDtypeStruct(pair_input.shape, BF),
            jax.ShapeDtypeStruct(pair_input.shape, BF),
            jax.ShapeDtypeStruct(w_in.shape, FL),
            jax.ShapeDtypeStruct(w_out.shape, FL),
            jax.ShapeDtypeStruct((8, C), FL),
        ),
        in_specs=[vmem] * 6,
        out_specs=[vmem] * 5,
        scratch_shapes=[
            pltpu.VMEM((6, LINE, rows, GROUP, length), BF),
            pltpu.VMEM((6, LINE, rows, GROUP, length), BF),
            pltpu.VMEM((6, GROUP, piece, C), BF),
            pltpu.VMEM((6, GROUP, piece, C), BF),
            pltpu.VMEM((GROUP * (piece + 1), C), FL),
            pltpu.VMEM((SIDE, SIDE, GROWS, C), BF),
            pltpu.VMEM((LINE, SIDE, GROWS, C), BF),
            pltpu.VMEM((SIDE, GROWS, C), BF),
            pltpu.VMEM((GROUP, GROWS, C), BF),
            pltpu.VMEM((GROWS, C), BF),
            pltpu.VMEM((SIDE, GROWS, C), BF),
            pltpu.VMEM((SIDE, SIDE, GROWS, C), BF),
            *[pltpu.VMEM(square, BF)] * 6,
            pltpu.VMEM((LINE * GROUP * CHUNKS[1][1], length), FL),
            pltpu.VMEM(held, FL),
            pltpu.VMEM((rows, 1, length), FL),
            pltpu.VMEM(held, BF),
            *[pltpu.VMEM(held, FL)] * 7,
            pltpu.VMEM(held, BF),
            pltpu.VMEM(held, BF),
            pltpu.VMEM((rows, 5 * C, length), BF),
            pltpu.VMEM((5 * C, C), BF),
            pltpu.VMEM((C, 5 * C), BF),
            pltpu.VMEM((C, C), BF),
            pltpu.VMEM((C, C), BF),
            pltpu.VMEM((C, C), FL),
            pltpu.VMEM((C, C), FL),
            pltpu.VMEM((C, C), BF),
            pltpu.VMEM((SIDE * SIDE * GROWS, C), BF),
            sem((6, 2)),
            sem((6, 2)),
            sem((6, 2)),
            sem((6, 2)),
            sem((8,)),
        ],
        compiler_params=pltpu.CompilerParams(
            collective_id=0, has_side_effects=True, vmem_limit_bytes=58 * 2**20
        ),
    )(pair_input, gain_in.reshape(1, C), w_in, w_out, product_gain.reshape(1, C), cotangent)
    return upd, gp, gwi, gwo, gains[0], gains[1]


def solution(mesh):
    return jax.shard_map(
        on_device,
        mesh=mesh,
        in_specs=(
            P(("crop", "res"), None, None),
            P(),
            P(),
            P(),
            P(),
            P(("crop", "res"), None, None),
        ),
        out_specs=(
            P(("crop", "res"), None, None),
            P(("crop", "res"), None, None),
            P("crop", None),
            P("crop", None),
            P("crop"),
            P("crop"),
        ),
        check_vma=False,
    )
```

```python
import functools

import jax
import jax.numpy as jnp
from jax import lax
from jax.experimental import pallas as pl
from jax.experimental.pallas import tpu as pltpu
from jax.sharding import PartitionSpec as P

EPS = 1e-05
FL = jnp.float32
BF = jnp.bfloat16
C = 128
LINE = 8
GROUP = 2 * LINE
GROWS = 16
SIDE = 7
ROUND = (1, 7, 2, 6, 3, 5, 4)
CHUNKS = ((0, 1), (1, 2), (3, 2))
ALL = range(len(CHUNKS))


def dot(a, b, dims=((1,), (0,))):
    return lax.dot_general(a, b, (dims, ((), ())), preferred_element_type=FL)


NT = ((1,), (1,))


def padded(count, tiles):
    return -(-(LINE * count * tiles) // 16) * 16


def sigmoid(x):
    return jax.nn.sigmoid(x)


def kernel(
    rows, length,
    z_ref, gain_in_ref, w_in_ref, w_out_ref, gain_out_ref, cot_ref,
    upd_ref, gp_ref, gwi_ref, gwo_ref, ggi_ref, ggo_ref,
    send1, recv1, send2, recv2, send_w, recv_w, mixed, swap, upd_v, gp_v,
    g_send, g_recv, h_send, h_recv, o_send, c_recv, d_recv,
    left_m, right_m, dprod_m, turned_m, order, order_t, wide,
    zhat, zinv, normed, p_l, s_l, p_r, s_r, s_g, cot_t, upd_t, xn, d_lin, d_proj,
    w_in_t, w_in_p, w_out_t, w_out_p, gain_in_c, gain_out_c, perm, grads,
    send_sem1, recv_sem1, send_sem2, recv_sem2, g_sems, out_sems,
):
    tiles = length // C

    def sizes(chunk):
        first, count = CHUNKS[chunk]
        base = LINE * GROUP * first
        return first, count, padded(count, tiles), LINE * count, base

    me = lax.axis_index("res")
    z = me // GROUP
    y = (me // 2) % LINE
    core = me % 2
    a = y + core * (z - y)
    b = z + core * (y - z)
    step_a = 2 + (GROUP - 2) * core
    step_b = GROUP - (GROUP - 2) * core

    def device(at_a, at_b, at_core):
        return at_a * step_a + at_b * step_b + at_core

    def remote(src, dst, on_send, on_recv, to):
        return pltpu.make_async_remote_copy(
            src_ref=src,
            dst_ref=dst,
            send_sem=on_send,
            recv_sem=on_recv,
            device_id={"res": to},
            device_id_type=pl.DeviceIdType.MESH,
        )

    other = device(a, b, 1 - core)
    barrier = pltpu.get_barrier_semaphore()

    def greet(to):
        pl.semaphore_signal(
            barrier, inc=1, device_id={"res": to}, device_id_type=pl.DeviceIdType.MESH
        )

    greet(other)
    for t in ROUND:
        for at_core in (0, 1):
            greet(device((a + t) % LINE, b, at_core))
            greet(device(a, (b + t) % LINE, at_core))

    def send_rows(stage, chunk):
        first, count = CHUNKS[chunk]
        part = pl.ds(first, count)
        for t in ROUND:
            at_a = (a + t) % LINE
            remote(
                send1.at[stage, at_a, part],
                recv1.at[stage, a, part],
                send_sem1.at[stage, chunk],
                recv_sem1.at[stage, chunk],
                device(at_a, b, core),
            ).start()
        recv1[stage, a, part] = send1[stage, a, part]

    def all_a(stage, chunk):
        first, count = CHUNKS[chunk]
        return remote(
            send1.at[stage, pl.ds(0, LINE - 1), pl.ds(first, count)],
            recv1.at[stage, pl.ds(0, LINE - 1), pl.ds(first, count)],
            send_sem1.at[stage, chunk],
            recv_sem1.at[stage, chunk],
            other,
        )

    def all_b(stage, chunk):
        out, into = pieces(stage, chunk)
        return remote(
            out.at[pl.ds(0, GROUP - 1)],
            into.at[pl.ds(0, GROUP - 1)],
            send_sem2.at[stage, chunk],
            recv_sem2.at[stage, chunk],
            other,
        )

    def pieces(stage, chunk):
        if CHUNKS[chunk][1] == 1:
            return send2.at[stage], recv2.at[stage]
        return send_w.at[stage, chunk - 1], recv_w.at[stage, chunk - 1]

    def swapped(value):
        return dot(swap[...], value.reshape(GROUP * GROUP, length)).astype(BF)

    def place(stage, row, value):
        value = value.astype(BF)
        for at in range(LINE):
            send1[stage, at, row] = value[at * GROUP : (at + 1) * GROUP]

    def relay_rows(stage, chunk):
        first, count, piece, _, _ = sizes(chunk)
        out, into = pieces(stage, chunk)
        stride = piece + 1
        all_a(stage, chunk).wait_recv()
        if count == 2:
            out[...] = swapped(recv1[stage, :, first : first + 2]).reshape(GROUP, GROUP, length)
        else:
            for at in range(LINE):
                block = recv1[stage, at, first].astype(FL)
                for tile in range(tiles):
                    mixed[pl.ds(at * tiles + tile, GROUP, stride=stride), :] = block[
                        :, tile * C : (tile + 1) * C
                    ]
            for q in range(GROUP):
                out[q] = mixed[q * stride : q * stride + piece, :].astype(BF)
        mine = b * 2 + core
        for t in (0,) + ROUND:
            at_b = (b + t) % LINE
            for turn in (0, 1):
                if t == 0 and turn == 0:
                    continue
                at_core = (core + turn) % 2
                remote(
                    out.at[at_b * 2 + at_core],
                    into.at[mine],
                    send_sem2.at[stage, chunk],
                    recv_sem2.at[stage, chunk],
                    device(a, at_b, at_core),
                ).start()
        into[mine] = out[mine]

    def take_channel(stage, chunk, into):
        first, count, piece, lot, base = sizes(chunk)
        all_b(stage, chunk).wait_recv()
        if count == 2:
            into[base : base + GROUP * lot, :] = pieces(stage, chunk)[1][...].reshape(
                GROUP * lot, length
            )
            return
        for slot in range(GROUP):
            mixed[slot * piece : (slot + 1) * piece, :] = recv2[stage, slot].astype(FL)
        for at in range(LINE):
            top = base + at * 2 * lot
            for tile in range(tiles):
                both = [
                    mixed[pl.ds((at * 2 + k) * piece + tile, lot, stride=tiles), :]
                    for k in (0, 1)
                ]
                into[top : top + 2 * lot, tile * C : (tile + 1) * C] = (
                    jnp.concatenate(both, axis=0).astype(BF)
                )

    def of(factor, chunk):
        _, _, _, lot, base = sizes(chunk)
        return factor[base : base + GROUP * lot, :]

    def send_channel(stage, chunk, whole):
        _, _, piece, lot, _ = sizes(chunk)
        out, into = pieces(stage, chunk)
        single = CHUNKS[chunk][1] == 1
        if single:
            wide[...] = whole
        else:
            out[...] = whole.astype(BF).reshape(GROUP, GROUP, length)
        for t in (0,) + ROUND:
            at_b = (b + t) % LINE
            if single:
                part = wide[pl.ds(pl.multiple_of(at_b * 2 * lot, GROUP), 2 * lot), :]
                for k in (0, 1):
                    for tile in range(tiles):
                        mixed[pl.ds(k * piece + tile, lot, stride=tiles), :] = part[
                            k * lot : (k + 1) * lot, tile * C : (tile + 1) * C
                        ]
            for k in (0, 1):
                if single:
                    out[at_b * 2 + k] = mixed[k * piece : (k + 1) * piece, :].astype(BF)
                to = (at_b * GROUP + y * 2) if k == 0 else (z * GROUP + at_b * 2 + 1)
                copy = remote(
                    out.at[at_b * 2 + k],
                    into.at[(z if k == 0 else y) * 2 + core],
                    send_sem2.at[stage, chunk],
                    recv_sem2.at[stage, chunk],
                    to,
                )
                if t == 0:

                    @pl.when(core == k)
                    def _():
                        into[at_b * 2 + k] = out[at_b * 2 + k]

                    @pl.when(core != k)
                    def _():
                        copy.start()

                else:
                    copy.start()

    def relay_channel(stage, chunk):
        first, count, piece, _, _ = sizes(chunk)
        stride = piece + 1
        all_b(stage, chunk).wait_recv()
        into = pieces(stage, chunk)[1]
        if count == 2:
            send1[stage, :, first : first + 2] = swapped(into[...]).reshape(LINE, 2, GROUP, length)
        else:
            for q in range(GROUP):
                mixed[q * stride : q * stride + piece, :] = into[q].astype(FL)
            for at in range(LINE):
                for tile in range(tiles):
                    send1[stage, at, first, :, tile * C : (tile + 1) * C] = mixed[
                        pl.ds(at * tiles + tile, GROUP, stride=stride), :
                    ].astype(BF)
        send_rows(stage, chunk)

    def take_row(stage, row):
        return jnp.concatenate([recv1[stage, at, row] for at in range(LINE)], axis=0).astype(FL)

    def chunk_rows(chunk):
        first, count = CHUNKS[chunk]
        return range(first, first + count)

    def iota(shape, dim):
        return lax.broadcasted_iota(jnp.int32, shape, dim)

    eye = (iota((C, C), 0) == iota((C, C), 1)).astype(BF)
    q = iota((C, C), 0)
    home = (q >> 4) * step_a + ((q >> 1) & 7) * step_b + (q & 1)
    perm_f = (home == iota((C, C), 1)).astype(FL)
    perm[...] = perm_f.astype(BF)
    def weights(block):
        sort = perm[...] if block < 4 else eye
        cols = slice(block * C, (block + 1) * C)
        w_in_t[cols, :] = dot(sort, w_in_ref[:, cols], NT).astype(BF)
        w_in_p[:, cols] = dot(w_in_ref[:, cols], sort, NT).astype(BF)

    weights(2)
    weights(3)
    gain_in_c[...] = jnp.transpose(jnp.broadcast_to(gain_in_ref[...], (C, C)))

    for chunk in ALL:
        for row in chunk_rows(chunk):
            zt = dot(eye, z_ref[row], NT)
            center = zt - jnp.mean(zt, axis=0, keepdims=True)
            inverse = lax.rsqrt(jnp.mean(center * center, axis=0, keepdims=True) + EPS)
            zh = center * inverse
            zhat[row] = zh
            zinv[row] = inverse
            normed[row] = (zh * gain_in_c[:, :1]).astype(BF)
            proj = dot(w_in_t[2 * C : 4 * C, :], normed[row])
            s_r[row] = sigmoid(proj[C:])
            p_r[row] = proj[:C]
            place(1, row, p_r[row] * s_r[row])
        if chunk == 0:
            pl.semaphore_wait(barrier, 4 * LINE - 3)
        send_rows(1, chunk)
    for block in (0, 1, 4):
        weights(block)
    for chunk in ALL:
        for row in chunk_rows(chunk):
            proj = dot(w_in_t[: 2 * C, :], normed[row])
            s_l[row] = sigmoid(proj[C:])
            p_l[row] = proj[:C]
            place(0, row, p_l[row] * s_l[row])
        send_rows(0, chunk)

    w_out_p[...] = dot(perm[...], w_out_ref[...]).astype(BF)
    w_out_t[...] = jnp.transpose(dot(perm[...], w_out_ref[...])).astype(BF)
    gain_out_c[...] = jnp.broadcast_to(
        jnp.sum(perm_f * gain_out_ref[...], axis=1, keepdims=True), (C, C)
    )
    mixed[...] = jnp.zeros(mixed.shape, FL)
    p = iota((1, GROUP * GROUP), 1)
    turned = (p & (GROUP - 1)) * GROUP + (p >> 4)
    swap[...] = (iota((GROUP * GROUP, GROUP * GROUP), 0) == turned).astype(FL).astype(BF)

    def natural(p):
        count = jnp.full(p.shape, float(CHUNKS[0][1]), FL)
        first = jnp.zeros(p.shape, FL)
        for start, size in CHUNKS[1:]:
            later = p >= LINE * GROUP * start
            count = jnp.where(later, float(size), count)
            first = jnp.where(later, float(start), first)
        pf = p.astype(FL) + 0.5 - first * (LINE * GROUP)
        at_b = jnp.floor(pf / (count * GROUP))
        pf = pf - at_b * (count * GROUP)
        at_core = jnp.floor(pf / (count * LINE))
        pf = pf - at_core * (count * LINE)
        at_a = jnp.floor(pf / count)
        row = pf - 0.5 - at_a * count + first
        at_z = at_b + at_core * (at_a - at_b)
        at_y = at_a + at_core * (at_b - at_a)
        return ((at_z * GROUP + at_y * 2 + at_core) * rows + row + 0.5).astype(jnp.int32)

    order[...] = (iota((length, length), 0) == natural(iota((1, length), 1))).astype(FL).astype(BF)
    order_t[...] = (
        (iota((length, length), 1) == natural(iota((length, 1), 0))).astype(FL).astype(BF)
    )

    for chunk in ALL:
        relay_rows(1, chunk)
    for row in range(rows):
        s_g[row] = sigmoid(dot(w_in_t[4 * C :, :], normed[row]))
    for chunk in ALL:
        relay_rows(0, chunk)
    for row in range(rows):
        cot_t[row] = dot(eye, cot_ref[row], NT)
    for chunk in ALL:
        take_channel(1, chunk, turned_m)
    right_m[...] = dot(order[...], turned_m[...]).astype(BF)
    for chunk in ALL:
        take_channel(0, chunk, left_m)
        send_channel(2, chunk, dot(of(left_m, chunk), right_m[...], NT))

    gg_parts = []

    def middle(chunk):
        all_a(2, chunk).wait_recv()
        gg_out = jnp.zeros((C, C), FL)
        for row in chunk_rows(chunk):
            prod = take_row(2, row)
            center = prod - jnp.mean(prod, axis=0, keepdims=True)
            inverse = lax.rsqrt(jnp.mean(center * center, axis=0, keepdims=True) + EPS)
            xh = center * inverse
            xn[row] = (xh * gain_out_c[:, :1]).astype(BF)
            lin = dot(w_out_t[...], xn[row])
            s = s_g[row]
            upd_t[row] = s * lin
            g = cot_t[row]
            d_lin[row] = (g * s).astype(BF)
            d_proj[row, 4 * C :, :] = (g * lin * s * (1.0 - s)).astype(BF)
            d_xn = dot(w_out_p[...], d_lin[row])
            both = d_xn * xh
            for tile in range(tiles):
                gg_out = gg_out + both[:, tile * C : (tile + 1) * C]
            h = d_xn * gain_out_c[:, :1]
            first = jnp.mean(h, axis=0, keepdims=True)
            second = jnp.mean(h * xh, axis=0, keepdims=True)
            place(3, row, inverse * (h - first - xh * second))
        send_rows(3, chunk)
        gg_parts.append(gg_out)

    def left_back(chunk):
        take_channel(3, chunk, dprod_m)
        send_channel(4, chunk, dot(of(dprod_m, chunk), right_m[...]))

    def right_back(chunk):
        send_channel(5, chunk, dot(of(turned_m, chunk), left_m[...]))

    relay_channel(2, 0)
    relay_channel(2, 1)
    middle(0)
    relay_channel(2, 2)
    middle(1)
    relay_rows(3, 0)
    middle(2)
    relay_rows(3, 1)
    left_back(0)
    relay_rows(3, 2)
    left_back(1)
    left_back(2)
    relay_channel(4, 0)
    turned_m[...] = dot(order_t[...], dprod_m[...], NT).astype(BF)
    right_back(0)
    relay_channel(4, 1)
    right_back(1)
    relay_channel(4, 2)
    right_back(2)
    gg_out = gg_parts[0] + gg_parts[1] + gg_parts[2]
    gw = jnp.zeros((C, C), FL)
    gw_gate = jnp.zeros((C, C), FL)
    for row in range(rows):
        gw = gw + dot(xn[row], d_lin[row], NT)
        gw_gate = gw_gate + dot(normed[row], d_proj[row, 4 * C :, :], NT)
    grads[4 * C : 5 * C, :] = gw_gate.astype(BF)
    grads[5 * C : 6 * C, :] = dot(perm[...], gw.astype(BF)).astype(BF)

    def leave(held, out, which, row):
        return pltpu.make_async_copy(held.at[row], out.at[row], out_sems.at[which, row])

    def write_update(picked):
        for row in picked:
            for tile in range(tiles):
                upd_v[row, tile * C : (tile + 1) * C, :] = jnp.transpose(
                    upd_t[row, :, tile * C : (tile + 1) * C]
                ).astype(BF)
            leave(upd_v, upd_ref, 0, row).start()

    def write_rows(picked):
        for row in picked:
            zh = zhat[row]
            h = p_l[row] * gain_in_c[:, :1]
            first = jnp.mean(h, axis=0, keepdims=True)
            second = jnp.mean(h * zh, axis=0, keepdims=True)
            out = zinv[row] * (h - first - zh * second)
            for tile in range(tiles):
                gp_v[row, tile * C : (tile + 1) * C, :] = jnp.transpose(
                    out[:, tile * C : (tile + 1) * C]
                ).astype(BF)
            leave(gp_v, gp_ref, 1, row).start()

    def factor_back(side, chunk, total):
        p_ref, s_ref = ((p_l, s_l), (p_r, s_r))[side]
        base = side * 2 * C
        all_a(4 + side, chunk).wait_recv()
        for row in chunk_rows(chunk):
            d = take_row(4 + side, row)
            s = s_ref[row]
            d_proj[row, base : base + C, :] = (d * s).astype(BF)
            d_proj[row, base + C : base + 2 * C, :] = (d * p_ref[row] * s * (1.0 - s)).astype(BF)
            total = total + dot(normed[row], d_proj[row, base : base + 2 * C, :], NT)
        return total

    def weights_back(side, total):
        base = side * 2 * C
        total = total.astype(BF)
        grads[base : base + C, :] = dot(total[:, :C], perm[...]).astype(BF)
        grads[base + C : base + 2 * C, :] = dot(total[:, C:], perm[...]).astype(BF)

    total = jnp.zeros((C, 2 * C), FL)
    write_update(range(0, 2))
    total = factor_back(0, 0, total)
    relay_channel(5, 0)
    total = factor_back(0, 1, total)
    relay_channel(5, 1)
    write_update(range(2, rows))
    total = factor_back(0, 2, total)
    weights_back(0, total)
    relay_channel(5, 2)
    total = jnp.zeros((C, 2 * C), FL)
    gg_in = jnp.zeros((C, C), FL)
    for chunk in ALL:
        total = factor_back(1, chunk, total)
        for row in chunk_rows(chunk):
            d_normed = dot(w_in_p[...], d_proj[row])
            p_l[row] = d_normed
            both = d_normed * zhat[row]
            for tile in range(tiles):
                gg_in = gg_in + both[:, tile * C : (tile + 1) * C]
        if chunk < 2:
            write_rows(chunk_rows(chunk))
    weights_back(1, total)

    gg_in = jnp.sum(jnp.transpose(gg_in), axis=0, keepdims=True)
    gg_out = jnp.sum(jnp.transpose(gg_out), axis=0, keepdims=True)
    gg_out = dot(jnp.broadcast_to(gg_out, (GROWS, C)).astype(BF), perm[...])
    line = iota((GROWS, C), 0)
    grads[6 * C :, :] = jnp.where(line == 0, jnp.broadcast_to(gg_in, (GROWS, C)), gg_out).astype(BF)

    def both_ways(u, v):
        return v + core * (u - v), u + core * (v - u)

    for u in range(SIDE):
        for v in range(SIDE):
            at = (u * SIDE + v) * GROWS
            g_send[both_ways(u, v)] = grads[at : at + GROWS, :]

    in_a = a < SIDE
    in_b = b < SIDE
    owner = jnp.logical_and(in_a, in_b)
    for t in ROUND:
        at_a = (a + t) % LINE

        @pl.when(at_a < SIDE)
        def _():
            remote(
                g_send.at[at_a], g_recv.at[a], g_sems.at[0], g_sems.at[1], device(at_a, b, core)
            ).start()

    def some(ref, count, on_send, on_recv):
        return remote(ref.at[pl.ds(0, count)], ref.at[pl.ds(0, count)], on_send, on_recv, other)

    mine = b * 2 + core

    @pl.when(in_a)
    def _():
        g_recv[a] = g_send[a]
        some(g_recv, LINE - 1, g_sems.at[0], g_sems.at[1]).wait_recv()
        h_send[...] = jnp.sum(g_recv[...].astype(FL), axis=0).astype(BF)
        for t in (0,) + ROUND:
            at_b = (b + t) % LINE
            for turn in (0, 1):
                if t == 0 and turn == 0:
                    continue
                at_core = (core + turn) % 2

                @pl.when(at_b < SIDE)
                def _():
                    remote(
                        h_send.at[at_b],
                        h_recv.at[mine],
                        g_sems.at[2],
                        g_sems.at[3],
                        device(a, at_b, at_core),
                    ).start()

    write_rows(range(3, 4))

    @pl.when(owner)
    def _():
        h_recv[mine] = h_send[b]
        some(h_recv, GROUP - 1, g_sems.at[2], g_sems.at[3]).wait_recv()
        total = jnp.sum(h_recv[...].astype(FL), axis=0) * (1.0 / length)
        o_send[...] = total.astype(BF)
        for t in ROUND:
            remote(
                o_send, c_recv.at[b], g_sems.at[4], g_sems.at[5], device(a, (b + t) % LINE, core)
            ).start()
        c_recv[b] = o_send[...]

    write_rows(range(4, rows))

    @pl.when(in_a)
    def _():
        @pl.when(in_b)
        def _():
            some(c_recv, SIDE - 1, g_sems.at[4], g_sems.at[5]).wait_recv()

        @pl.when(jnp.logical_not(in_b))
        def _():
            some(c_recv, SIDE, g_sems.at[4], g_sems.at[5]).wait_recv()

        for t in ROUND:
            remote(
                c_recv, d_recv.at[a], g_sems.at[6], g_sems.at[7], device((a + t) % LINE, b, core)
            ).start()
        d_recv[a] = c_recv[...]
        some(d_recv, SIDE - 1, g_sems.at[6], g_sems.at[7]).wait_recv()

    @pl.when(jnp.logical_not(in_a))
    def _():
        some(d_recv, SIDE, g_sems.at[6], g_sems.at[7]).wait_recv()

    per = C // GROWS
    for u in range(SIDE):
        for v in range(SIDE):
            block, at = divmod(u * SIDE + v, per)
            value = d_recv[both_ways(u, v)].astype(FL)
            at = at * GROWS
            if block < 5:
                gwi_ref[at : at + GROWS, block * C : (block + 1) * C] = value
            elif block == 5:
                gwo_ref[at : at + GROWS, :] = value
            else:
                ggi_ref[...] = value[0:1]
                ggo_ref[...] = value[1:2]

    @pl.when(in_a)
    def _():
        some(g_send, SIDE - 1, g_sems.at[0], g_sems.at[1]).wait_send()
        some(g_recv, LINE - 1, g_sems.at[6], g_sems.at[7]).wait_send()

        @pl.when(in_b)
        def _():
            some(h_recv, GROUP - 3, g_sems.at[2], g_sems.at[3]).wait_send()
            some(h_recv, LINE - 1, g_sems.at[4], g_sems.at[5]).wait_send()

        @pl.when(jnp.logical_not(in_b))
        def _():
            some(h_recv, GROUP - 2, g_sems.at[2], g_sems.at[3]).wait_send()

    @pl.when(jnp.logical_not(in_a))
    def _():
        some(g_send, SIDE, g_sems.at[0], g_sems.at[1]).wait_send()

    for stage in range(6):
        for chunk in ALL:
            all_a(stage, chunk).wait_send()
            all_b(stage, chunk).wait_send()
    for row in range(rows):
        leave(upd_v, upd_ref, 0, row).wait()
        leave(gp_v, gp_ref, 1, row).wait()


def write(rows, *refs):
    into, out = refs[-2:]
    pairs = []
    for src, held, dst in zip(refs[:6], refs[12:18], refs[6:12]):
        if len(src.shape) == 3:
            pairs += [(src.at[row], held.at[row], dst.at[row]) for row in range(rows)]
        else:
            pairs.append((src, held, dst))
    reads = [pltpu.make_async_copy(s, h, into.at[i]) for i, (s, h, _) in enumerate(pairs)]
    writes = [pltpu.make_async_copy(h, d, out.at[i]) for i, (_, h, d) in enumerate(pairs)]
    for copy in reads:
        copy.start()
    for read, copy in zip(reads, writes):
        read.wait()
        copy.start()
    for copy in writes:
        copy.wait()


def on_device(pair_input, gain_in, w_in, w_out, product_gain, cotangent):
    rows, length, width = pair_input.shape
    piece = padded(1, length // C)
    pairs = len(CHUNKS) - 1
    anywhere = pl.BlockSpec(memory_space=pl.ANY)
    held = (rows, C, length)
    square = (length, length)
    vmem = pl.BlockSpec(memory_space=pltpu.VMEM)
    sem = pltpu.SemaphoreType.DMA
    shapes = (
        jax.ShapeDtypeStruct(pair_input.shape, BF),
        jax.ShapeDtypeStruct(pair_input.shape, BF),
        jax.ShapeDtypeStruct(w_in.shape, FL),
        jax.ShapeDtypeStruct(w_out.shape, FL),
        jax.ShapeDtypeStruct((1, C), FL),
        jax.ShapeDtypeStruct((1, C), FL),
    )
    results = pl.pallas_call(
        functools.partial(kernel, rows, length),
        out_shape=shapes,
        in_specs=[vmem] * 6,
        out_specs=[anywhere] * 2 + [vmem] * 4,
        scratch_shapes=[
            pltpu.VMEM((6, LINE, rows, GROUP, length), BF),
            pltpu.VMEM((6, LINE, rows, GROUP, length), BF),
            pltpu.VMEM((6, GROUP, piece, C), BF),
            pltpu.VMEM((6, GROUP, piece, C), BF),
            pltpu.VMEM((6, pairs, GROUP, GROUP, length), BF),
            pltpu.VMEM((6, pairs, GROUP, GROUP, length), BF),
            pltpu.VMEM((GROUP * (piece + 1), C), FL),
            pltpu.VMEM((GROUP * GROUP, GROUP * GROUP), BF),
            pltpu.VMEM(pair_input.shape, BF),
            pltpu.VMEM(pair_input.shape, BF),
            pltpu.VMEM((SIDE, SIDE, GROWS, C), BF),
            pltpu.VMEM((LINE, SIDE, GROWS, C), BF),
            pltpu.VMEM((SIDE, GROWS, C), BF),
            pltpu.VMEM((GROUP, GROWS, C), BF),
            pltpu.VMEM((GROWS, C), BF),
            pltpu.VMEM((SIDE, GROWS, C), BF),
            pltpu.VMEM((SIDE, SIDE, GROWS, C), BF),
            *[pltpu.VMEM(square, BF)] * 6,
            pltpu.VMEM((LINE * GROUP, length), FL),
            pltpu.VMEM(held, FL),
            pltpu.VMEM((rows, 1, length), FL),
            pltpu.VMEM(held, BF),
            *[pltpu.VMEM(held, FL)] * 7,
            pltpu.VMEM(held, BF),
            pltpu.VMEM(held, BF),
            pltpu.VMEM((rows, 5 * C, length), BF),
            pltpu.VMEM((5 * C, C), BF),
            pltpu.VMEM((C, 5 * C), BF),
            pltpu.VMEM((C, C), BF),
            pltpu.VMEM((C, C), BF),
            pltpu.VMEM((C, C), FL),
            pltpu.VMEM((C, C), FL),
            pltpu.VMEM((C, C), BF),
            pltpu.VMEM((SIDE * SIDE * GROWS, C), BF),
            sem((6, len(CHUNKS))),
            sem((6, len(CHUNKS))),
            sem((6, len(CHUNKS))),
            sem((6, len(CHUNKS))),
            sem((8,)),
            sem((2, rows)),
        ],
        compiler_params=pltpu.CompilerParams(
            collective_id=0, has_side_effects=True, vmem_limit_bytes=58 * 2**20
        ),
    )(pair_input, gain_in.reshape(1, C), w_in, w_out, product_gain.reshape(1, C), cotangent)
    upd, gp, gwi, gwo, ggi, ggo = pl.pallas_call(
        functools.partial(write, rows),
        out_shape=shapes,
        in_specs=[anywhere] * 6,
        out_specs=[anywhere] * 6,
        scratch_shapes=[pltpu.VMEM(shape.shape, shape.dtype) for shape in shapes]
        + [sem((2 * rows + 4,)), sem((2 * rows + 4,))],
        compiler_params=pltpu.CompilerParams(vmem_limit_bytes=60 * 2**20),
    )(*results)
    return upd, gp, gwi, gwo, ggi.reshape(C), ggo.reshape(C)


def solution(mesh):
    return jax.shard_map(
        on_device,
        mesh=mesh,
        in_specs=(
            P(("crop", "res"), None, None),
            P(),
            P(),
            P(),
            P(),
            P(("crop", "res"), None, None),
        ),
        out_specs=(
            P(("crop", "res"), None, None),
            P(("crop", "res"), None, None),
            P("crop", None),
            P("crop", None),
            P("crop"),
            P("crop"),
        ),
        check_vma=False,
    )
```

```python
import functools

import jax
import jax.numpy as jnp
from jax import lax
from jax.experimental import pallas as pl
from jax.experimental.pallas import tpu as pltpu
from jax.sharding import PartitionSpec as P

EPS = 1e-05
FL = jnp.float32
BF = jnp.bfloat16
C = 128
LINE = 8
GROUP = 2 * LINE
GROWS = 16
SIDE = 7
ROUND = (4, 3, 5, 2, 6, 1, 7)
CHUNKS = ((0, 1), (1, 2), (3, 2))
ALL = range(len(CHUNKS))
LATE = (1, 2, 0)


def dot(a, b, dims=((1,), (0,))):
    return lax.dot_general(a, b, (dims, ((), ())), preferred_element_type=FL)


NT = ((1,), (1,))


def padded(count, tiles):
    return -(-(LINE * count * tiles) // 16) * 16


def sigmoid(x):
    return jax.nn.sigmoid(x)


def kernel(
    rows, length,
    z_ref, gain_in_ref, w_in_ref, w_out_ref, gain_out_ref, cot_ref,
    upd_ref, gp_ref, gwi_ref, gwo_ref, ggi_ref, ggo_ref,
    send1, recv1, send2, recv2, send_w, recv_w, mixed, swap, upd_v, gp_v,
    g_send, g_recv, h_send, h_recv, o_send, c_recv, d_recv,
    left_m, right_m, dprod_m, turned_m, order, order_t, wide,
    zhat, zinv, normed, p_l, s_l, p_r, s_r, s_g, cot_t, upd_t, xn, d_lin, d_proj,
    w_in_t, w_in_p, w_out_t, w_out_p, gain_in_c, gain_out_c, perm, grads,
    send_sem1, recv_sem1, send_sem2, recv_sem2, g_sems, out_sems,
):
    tiles = length // C

    def sizes(chunk):
        first, count = CHUNKS[chunk]
        base = LINE * GROUP * first
        return first, count, padded(count, tiles), LINE * count, base

    me = lax.axis_index("res")
    z = me // GROUP
    y = (me // 2) % LINE
    core = me % 2
    a = y + core * (z - y)
    b = z + core * (y - z)
    step_a = 2 + (GROUP - 2) * core
    step_b = GROUP - (GROUP - 2) * core

    def device(at_a, at_b, at_core):
        return at_a * step_a + at_b * step_b + at_core

    def remote(src, dst, on_send, on_recv, to):
        return pltpu.make_async_remote_copy(
            src_ref=src,
            dst_ref=dst,
            send_sem=on_send,
            recv_sem=on_recv,
            device_id={"res": to},
            device_id_type=pl.DeviceIdType.MESH,
        )

    other = device(a, b, 1 - core)
    barrier = pltpu.get_barrier_semaphore()

    def greet(to):
        pl.semaphore_signal(
            barrier, inc=1, device_id={"res": to}, device_id_type=pl.DeviceIdType.MESH
        )

    greet(other)
    for t in ROUND:
        for at_core in (0, 1):
            greet(device((a + t) % LINE, b, at_core))
            greet(device(a, (b + t) % LINE, at_core))

    def send_rows(stage, chunk):
        first, count = CHUNKS[chunk]
        part = pl.ds(first, count)
        for t in ROUND:
            at_a = (a + t) % LINE
            remote(
                send1.at[stage, at_a, part],
                recv1.at[stage, a, part],
                send_sem1.at[stage, chunk],
                recv_sem1.at[stage, chunk],
                device(at_a, b, core),
            ).start()
        recv1[stage, a, part] = send1[stage, a, part]

    def all_a(stage, chunk):
        first, count = CHUNKS[chunk]
        return remote(
            send1.at[stage, pl.ds(0, LINE - 1), pl.ds(first, count)],
            recv1.at[stage, pl.ds(0, LINE - 1), pl.ds(first, count)],
            send_sem1.at[stage, chunk],
            recv_sem1.at[stage, chunk],
            other,
        )

    def all_b(stage, chunk):
        out, into = pieces(stage, chunk)
        return remote(
            out.at[pl.ds(0, GROUP - 1)],
            into.at[pl.ds(0, GROUP - 1)],
            send_sem2.at[stage, chunk],
            recv_sem2.at[stage, chunk],
            other,
        )

    def pieces(stage, chunk):
        if CHUNKS[chunk][1] == 1:
            return send2.at[stage], recv2.at[stage]
        return send_w.at[stage, chunk - 1], recv_w.at[stage, chunk - 1]

    def swapped(value):
        return dot(swap[...], value.reshape(GROUP * GROUP, length)).astype(BF)

    def place(stage, row, value):
        value = value.astype(BF)
        for at in range(LINE):
            send1[stage, at, row] = value[at * GROUP : (at + 1) * GROUP]

    def relay_rows(stage, chunk):
        first, count, piece, _, _ = sizes(chunk)
        out, into = pieces(stage, chunk)
        stride = piece + 1
        all_a(stage, chunk).wait_recv()
        if count == 2:
            out[...] = swapped(recv1[stage, :, first : first + 2]).reshape(GROUP, GROUP, length)
        else:
            for at in range(LINE):
                block = recv1[stage, at, first].astype(FL)
                for tile in range(tiles):
                    mixed[pl.ds(at * tiles + tile, GROUP, stride=stride), :] = block[
                        :, tile * C : (tile + 1) * C
                    ]
            for q in range(GROUP):
                out[q] = mixed[q * stride : q * stride + piece, :].astype(BF)
        mine = b * 2 + core
        for t in ROUND + (0,):
            at_b = (b + t) % LINE
            for turn in (0, 1):
                if t == 0 and turn == 0:
                    continue
                at_core = (core + turn) % 2
                remote(
                    out.at[at_b * 2 + at_core],
                    into.at[mine],
                    send_sem2.at[stage, chunk],
                    recv_sem2.at[stage, chunk],
                    device(a, at_b, at_core),
                ).start()
        into[mine] = out[mine]

    def take_channel(stage, chunk, into):
        first, count, piece, lot, base = sizes(chunk)
        all_b(stage, chunk).wait_recv()
        if count == 2:
            into[base : base + GROUP * lot, :] = pieces(stage, chunk)[1][...].reshape(
                GROUP * lot, length
            )
            return
        for slot in range(GROUP):
            mixed[slot * piece : (slot + 1) * piece, :] = recv2[stage, slot].astype(FL)
        for at in range(LINE):
            top = base + at * 2 * lot
            for tile in range(tiles):
                both = [
                    mixed[pl.ds((at * 2 + k) * piece + tile, lot, stride=tiles), :]
                    for k in (0, 1)
                ]
                into[top : top + 2 * lot, tile * C : (tile + 1) * C] = (
                    jnp.concatenate(both, axis=0).astype(BF)
                )

    def of(factor, chunk):
        _, _, _, lot, base = sizes(chunk)
        return factor[base : base + GROUP * lot, :]

    def send_channel(stage, chunk, whole):
        _, _, piece, lot, _ = sizes(chunk)
        out, into = pieces(stage, chunk)
        single = CHUNKS[chunk][1] == 1
        if single:
            wide[...] = whole
        else:
            out[...] = whole.astype(BF).reshape(GROUP, GROUP, length)
        for t in ROUND + (0,):
            at_b = (b + t) % LINE
            if single:
                part = wide[pl.ds(pl.multiple_of(at_b * 2 * lot, GROUP), 2 * lot), :]
                for k in (0, 1):
                    for tile in range(tiles):
                        mixed[pl.ds(k * piece + tile, lot, stride=tiles), :] = part[
                            k * lot : (k + 1) * lot, tile * C : (tile + 1) * C
                        ]
            for k in (0, 1):
                if single:
                    out[at_b * 2 + k] = mixed[k * piece : (k + 1) * piece, :].astype(BF)
                to = (at_b * GROUP + y * 2) if k == 0 else (z * GROUP + at_b * 2 + 1)
                copy = remote(
                    out.at[at_b * 2 + k],
                    into.at[(z if k == 0 else y) * 2 + core],
                    send_sem2.at[stage, chunk],
                    recv_sem2.at[stage, chunk],
                    to,
                )
                if t == 0:

                    @pl.when(core == k)
                    def _():
                        into[at_b * 2 + k] = out[at_b * 2 + k]

                    @pl.when(core != k)
                    def _():
                        copy.start()

                else:
                    copy.start()

    def relay_channel(stage, chunk):
        first, count, piece, _, _ = sizes(chunk)
        stride = piece + 1
        all_b(stage, chunk).wait_recv()
        into = pieces(stage, chunk)[1]
        if count == 2:
            send1[stage, :, first : first + 2] = swapped(into[...]).reshape(LINE, 2, GROUP, length)
        else:
            for q in range(GROUP):
                mixed[q * stride : q * stride + piece, :] = into[q].astype(FL)
            for at in range(LINE):
                for tile in range(tiles):
                    send1[stage, at, first, :, tile * C : (tile + 1) * C] = mixed[
                        pl.ds(at * tiles + tile, GROUP, stride=stride), :
                    ].astype(BF)
        send_rows(stage, chunk)

    def take_row(stage, row):
        return jnp.concatenate([recv1[stage, at, row] for at in range(LINE)], axis=0).astype(FL)

    def chunk_rows(chunk):
        first, count = CHUNKS[chunk]
        return range(first, first + count)

    def iota(shape, dim):
        return lax.broadcasted_iota(jnp.int32, shape, dim)

    eye = (iota((C, C), 0) == iota((C, C), 1)).astype(BF)
    q = iota((C, C), 0)
    home = (q >> 4) * step_a + ((q >> 1) & 7) * step_b + (q & 1)
    perm_f = (home == iota((C, C), 1)).astype(FL)
    perm[...] = perm_f.astype(BF)
    def weights(block):
        sort = perm[...] if block < 4 else eye
        cols = slice(block * C, (block + 1) * C)
        w_in_t[cols, :] = dot(sort, w_in_ref[:, cols], NT).astype(BF)
        w_in_p[:, cols] = dot(w_in_ref[:, cols], sort, NT).astype(BF)

    weights(2)
    weights(3)
    gain_in_c[...] = jnp.transpose(jnp.broadcast_to(gain_in_ref[...], (C, C)))

    for chunk in ALL:
        for row in chunk_rows(chunk):
            zt = dot(eye, z_ref[row], NT)
            center = zt - jnp.mean(zt, axis=0, keepdims=True)
            inverse = lax.rsqrt(jnp.mean(center * center, axis=0, keepdims=True) + EPS)
            zh = center * inverse
            zhat[row] = zh
            zinv[row] = inverse
            normed[row] = (zh * gain_in_c[:, :1]).astype(BF)
            proj = dot(w_in_t[2 * C : 4 * C, :], normed[row])
            s_r[row] = sigmoid(proj[C:])
            p_r[row] = proj[:C]
            place(1, row, p_r[row] * s_r[row])
        if chunk == 0:
            pl.semaphore_wait(barrier, 4 * LINE - 3)
        send_rows(1, chunk)
    for block in (0, 1, 4):
        weights(block)
    for chunk in LATE:
        for row in chunk_rows(chunk):
            proj = dot(w_in_t[: 2 * C, :], normed[row])
            s_l[row] = sigmoid(proj[C:])
            p_l[row] = proj[:C]
            place(0, row, p_l[row] * s_l[row])
        send_rows(0, chunk)

    w_out_p[...] = dot(perm[...], w_out_ref[...]).astype(BF)
    w_out_t[...] = jnp.transpose(dot(perm[...], w_out_ref[...])).astype(BF)
    gain_out_c[...] = jnp.broadcast_to(
        jnp.sum(perm_f * gain_out_ref[...], axis=1, keepdims=True), (C, C)
    )
    mixed[...] = jnp.zeros(mixed.shape, FL)
    p = iota((1, GROUP * GROUP), 1)
    turned = (p & (GROUP - 1)) * GROUP + (p >> 4)
    swap[...] = (iota((GROUP * GROUP, GROUP * GROUP), 0) == turned).astype(FL).astype(BF)

    def natural(p):
        count = jnp.full(p.shape, float(CHUNKS[0][1]), FL)
        first = jnp.zeros(p.shape, FL)
        for start, size in CHUNKS[1:]:
            later = p >= LINE * GROUP * start
            count = jnp.where(later, float(size), count)
            first = jnp.where(later, float(start), first)
        pf = p.astype(FL) + 0.5 - first * (LINE * GROUP)
        at_b = jnp.floor(pf / (count * GROUP))
        pf = pf - at_b * (count * GROUP)
        at_core = jnp.floor(pf / (count * LINE))
        pf = pf - at_core * (count * LINE)
        at_a = jnp.floor(pf / count)
        row = pf - 0.5 - at_a * count + first
        at_z = at_b + at_core * (at_a - at_b)
        at_y = at_a + at_core * (at_b - at_a)
        return ((at_z * GROUP + at_y * 2 + at_core) * rows + row + 0.5).astype(jnp.int32)

    order[...] = (iota((length, length), 0) == natural(iota((1, length), 1))).astype(FL).astype(BF)
    order_t[...] = (
        (iota((length, length), 1) == natural(iota((length, 1), 0))).astype(FL).astype(BF)
    )

    for chunk in ALL:
        relay_rows(1, chunk)
    for row in range(rows):
        s_g[row] = sigmoid(dot(w_in_t[4 * C :, :], normed[row]))
    for chunk in LATE:
        relay_rows(0, chunk)
    for row in range(rows):
        cot_t[row] = dot(eye, cot_ref[row], NT)
    for chunk in ALL:
        take_channel(1, chunk, turned_m)
    right_m[...] = dot(order[...], turned_m[...]).astype(BF)
    for chunk in LATE:
        take_channel(0, chunk, left_m)
        send_channel(2, chunk, dot(of(left_m, chunk), right_m[...], NT))

    gg_parts = []

    def middle(chunk):
        all_a(2, chunk).wait_recv()
        gg_out = jnp.zeros((C, C), FL)
        for row in chunk_rows(chunk):
            prod = take_row(2, row)
            center = prod - jnp.mean(prod, axis=0, keepdims=True)
            inverse = lax.rsqrt(jnp.mean(center * center, axis=0, keepdims=True) + EPS)
            xh = center * inverse
            xn[row] = (xh * gain_out_c[:, :1]).astype(BF)
            lin = dot(w_out_t[...], xn[row])
            s = s_g[row]
            upd_t[row] = s * lin
            g = cot_t[row]
            d_lin[row] = (g * s).astype(BF)
            d_proj[row, 4 * C :, :] = (g * lin * s * (1.0 - s)).astype(BF)
            d_xn = dot(w_out_p[...], d_lin[row])
            both = d_xn * xh
            for tile in range(tiles):
                gg_out = gg_out + both[:, tile * C : (tile + 1) * C]
            h = d_xn * gain_out_c[:, :1]
            first = jnp.mean(h, axis=0, keepdims=True)
            second = jnp.mean(h * xh, axis=0, keepdims=True)
            place(3, row, inverse * (h - first - xh * second))
        send_rows(3, chunk)
        gg_parts.append(gg_out)

    def left_back(chunk):
        take_channel(3, chunk, dprod_m)
        send_channel(4, chunk, dot(of(dprod_m, chunk), right_m[...]))

    def right_back(chunk):
        send_channel(5, chunk, dot(of(turned_m, chunk), left_m[...]))

    c0, c1, c2 = LATE
    relay_channel(2, c0)
    relay_channel(2, c1)
    middle(c0)
    relay_channel(2, c2)
    middle(c1)
    relay_rows(3, c0)
    middle(c2)
    relay_rows(3, c1)
    left_back(c0)
    relay_rows(3, c2)
    left_back(c1)
    left_back(c2)
    relay_channel(4, c0)
    turned_m[...] = dot(order_t[...], dprod_m[...], NT).astype(BF)
    right_back(c0)
    relay_channel(4, c1)
    right_back(c1)
    relay_channel(4, c2)
    right_back(c2)
    gg_out = gg_parts[0] + gg_parts[1] + gg_parts[2]
    gw = jnp.zeros((C, C), FL)
    gw_gate = jnp.zeros((C, C), FL)
    for row in range(rows):
        gw = gw + dot(xn[row], d_lin[row], NT)
        gw_gate = gw_gate + dot(normed[row], d_proj[row, 4 * C :, :], NT)
    grads[4 * C : 5 * C, :] = gw_gate.astype(BF)
    grads[5 * C : 6 * C, :] = dot(perm[...], gw.astype(BF)).astype(BF)

    def leave(held, out, which, row):
        return pltpu.make_async_copy(held.at[row], out.at[row], out_sems.at[which, row])

    def write_update(picked):
        for row in picked:
            for tile in range(tiles):
                upd_v[row, tile * C : (tile + 1) * C, :] = jnp.transpose(
                    upd_t[row, :, tile * C : (tile + 1) * C]
                ).astype(BF)
            leave(upd_v, upd_ref, 0, row).start()

    def write_rows(picked):
        for row in picked:
            zh = zhat[row]
            h = p_l[row] * gain_in_c[:, :1]
            first = jnp.mean(h, axis=0, keepdims=True)
            second = jnp.mean(h * zh, axis=0, keepdims=True)
            out = zinv[row] * (h - first - zh * second)
            for tile in range(tiles):
                gp_v[row, tile * C : (tile + 1) * C, :] = jnp.transpose(
                    out[:, tile * C : (tile + 1) * C]
                ).astype(BF)
            leave(gp_v, gp_ref, 1, row).start()

    def factor_back(side, chunk, total):
        p_ref, s_ref = ((p_l, s_l), (p_r, s_r))[side]
        base = side * 2 * C
        all_a(4 + side, chunk).wait_recv()
        for row in chunk_rows(chunk):
            d = take_row(4 + side, row)
            s = s_ref[row]
            d_proj[row, base : base + C, :] = (d * s).astype(BF)
            d_proj[row, base + C : base + 2 * C, :] = (d * p_ref[row] * s * (1.0 - s)).astype(BF)
            total = total + dot(normed[row], d_proj[row, base : base + 2 * C, :], NT)
        return total

    def weights_back(side, total):
        base = side * 2 * C
        total = total.astype(BF)
        grads[base : base + C, :] = dot(total[:, :C], perm[...]).astype(BF)
        grads[base + C : base + 2 * C, :] = dot(total[:, C:], perm[...]).astype(BF)

    total = jnp.zeros((C, 2 * C), FL)
    write_update(range(0, 2))
    total = factor_back(0, c0, total)
    relay_channel(5, c0)
    total = factor_back(0, c1, total)
    relay_channel(5, c1)
    write_update(range(2, rows))
    total = factor_back(0, c2, total)
    weights_back(0, total)
    relay_channel(5, c2)
    total = jnp.zeros((C, 2 * C), FL)
    gg_in = jnp.zeros((C, C), FL)
    for chunk in LATE:
        total = factor_back(1, chunk, total)
        for row in chunk_rows(chunk):
            d_normed = dot(w_in_p[...], d_proj[row])
            p_l[row] = d_normed
            both = d_normed * zhat[row]
            for tile in range(tiles):
                gg_in = gg_in + both[:, tile * C : (tile + 1) * C]
        if chunk != c2:
            write_rows(chunk_rows(chunk))
    weights_back(1, total)

    gg_in = jnp.sum(jnp.transpose(gg_in), axis=0, keepdims=True)
    gg_out = jnp.sum(jnp.transpose(gg_out), axis=0, keepdims=True)
    gg_out = dot(jnp.broadcast_to(gg_out, (GROWS, C)).astype(BF), perm[...])
    line = iota((GROWS, C), 0)
    grads[6 * C :, :] = jnp.where(line == 0, jnp.broadcast_to(gg_in, (GROWS, C)), gg_out).astype(BF)

    def both_ways(u, v):
        return v + core * (u - v), u + core * (v - u)

    for u in range(SIDE):
        for v in range(SIDE):
            at = (u * SIDE + v) * GROWS
            g_send[both_ways(u, v)] = grads[at : at + GROWS, :]

    in_a = a < SIDE
    in_b = b < SIDE
    owner = jnp.logical_and(in_a, in_b)
    for t in ROUND:
        at_a = (a + t) % LINE

        @pl.when(at_a < SIDE)
        def _():
            remote(
                g_send.at[at_a], g_recv.at[a], g_sems.at[0], g_sems.at[1], device(at_a, b, core)
            ).start()

    def some(ref, count, on_send, on_recv):
        return remote(ref.at[pl.ds(0, count)], ref.at[pl.ds(0, count)], on_send, on_recv, other)

    write_rows(chunk_rows(c2))
    mine = b * 2 + core

    @pl.when(in_a)
    def _():
        g_recv[a] = g_send[a]
        some(g_recv, LINE - 1, g_sems.at[0], g_sems.at[1]).wait_recv()
        h_send[...] = jnp.sum(g_recv[...].astype(FL), axis=0).astype(BF)
        for t in ROUND + (0,):
            at_b = (b + t) % LINE
            for turn in (0, 1):
                if t == 0 and turn == 0:
                    continue
                at_core = (core + turn) % 2

                @pl.when(at_b < SIDE)
                def _():
                    remote(
                        h_send.at[at_b],
                        h_recv.at[mine],
                        g_sems.at[2],
                        g_sems.at[3],
                        device(a, at_b, at_core),
                    ).start()


    @pl.when(owner)
    def _():
        h_recv[mine] = h_send[b]
        some(h_recv, GROUP - 1, g_sems.at[2], g_sems.at[3]).wait_recv()
        total = jnp.sum(h_recv[...].astype(FL), axis=0) * (1.0 / length)
        o_send[...] = total.astype(BF)
        for t in ROUND:
            remote(
                o_send, c_recv.at[b], g_sems.at[4], g_sems.at[5], device(a, (b + t) % LINE, core)
            ).start()
        c_recv[b] = o_send[...]


    @pl.when(in_a)
    def _():
        @pl.when(in_b)
        def _():
            some(c_recv, SIDE - 1, g_sems.at[4], g_sems.at[5]).wait_recv()

        @pl.when(jnp.logical_not(in_b))
        def _():
            some(c_recv, SIDE, g_sems.at[4], g_sems.at[5]).wait_recv()

        for t in ROUND:
            remote(
                c_recv, d_recv.at[a], g_sems.at[6], g_sems.at[7], device((a + t) % LINE, b, core)
            ).start()
        d_recv[a] = c_recv[...]
        some(d_recv, SIDE - 1, g_sems.at[6], g_sems.at[7]).wait_recv()

    @pl.when(jnp.logical_not(in_a))
    def _():
        some(d_recv, SIDE, g_sems.at[6], g_sems.at[7]).wait_recv()

    per = C // GROWS
    for u in range(SIDE):
        for v in range(SIDE):
            block, at = divmod(u * SIDE + v, per)
            value = d_recv[both_ways(u, v)].astype(FL)
            at = at * GROWS
            if block < 5:
                gwi_ref[at : at + GROWS, block * C : (block + 1) * C] = value
            elif block == 5:
                gwo_ref[at : at + GROWS, :] = value
            else:
                ggi_ref[...] = value[0:1]
                ggo_ref[...] = value[1:2]

    @pl.when(in_a)
    def _():
        some(g_send, SIDE - 1, g_sems.at[0], g_sems.at[1]).wait_send()
        some(g_recv, LINE - 1, g_sems.at[6], g_sems.at[7]).wait_send()

        @pl.when(in_b)
        def _():
            some(h_recv, GROUP - 3, g_sems.at[2], g_sems.at[3]).wait_send()
            some(h_recv, LINE - 1, g_sems.at[4], g_sems.at[5]).wait_send()

        @pl.when(jnp.logical_not(in_b))
        def _():
            some(h_recv, GROUP - 2, g_sems.at[2], g_sems.at[3]).wait_send()

    @pl.when(jnp.logical_not(in_a))
    def _():
        some(g_send, SIDE, g_sems.at[0], g_sems.at[1]).wait_send()

    for stage in range(6):
        for chunk in ALL:
            all_a(stage, chunk).wait_send()
            all_b(stage, chunk).wait_send()
    for row in range(rows):
        leave(upd_v, upd_ref, 0, row).wait()
        leave(gp_v, gp_ref, 1, row).wait()


def write(rows, *refs):
    into, out = refs[-2:]
    pairs = []
    for src, held, dst in zip(refs[:6], refs[12:18], refs[6:12]):
        if len(src.shape) == 3:
            pairs += [(src.at[row], held.at[row], dst.at[row]) for row in range(rows)]
        else:
            pairs.append((src, held, dst))
    reads = [pltpu.make_async_copy(s, h, into.at[i]) for i, (s, h, _) in enumerate(pairs)]
    writes = [pltpu.make_async_copy(h, d, out.at[i]) for i, (_, h, d) in enumerate(pairs)]
    for copy in reads:
        copy.start()
    for read, copy in zip(reads, writes):
        read.wait()
        copy.start()
    for copy in writes:
        copy.wait()


def on_device(pair_input, gain_in, w_in, w_out, product_gain, cotangent):
    rows, length, width = pair_input.shape
    piece = padded(1, length // C)
    pairs = len(CHUNKS) - 1
    anywhere = pl.BlockSpec(memory_space=pl.ANY)
    held = (rows, C, length)
    square = (length, length)
    vmem = pl.BlockSpec(memory_space=pltpu.VMEM)
    sem = pltpu.SemaphoreType.DMA
    shapes = (
        jax.ShapeDtypeStruct(pair_input.shape, BF),
        jax.ShapeDtypeStruct(pair_input.shape, BF),
        jax.ShapeDtypeStruct(w_in.shape, FL),
        jax.ShapeDtypeStruct(w_out.shape, FL),
        jax.ShapeDtypeStruct((1, C), FL),
        jax.ShapeDtypeStruct((1, C), FL),
    )
    results = pl.pallas_call(
        functools.partial(kernel, rows, length),
        out_shape=shapes,
        in_specs=[vmem] * 6,
        out_specs=[anywhere] * 2 + [vmem] * 4,
        scratch_shapes=[
            pltpu.VMEM((6, LINE, rows, GROUP, length), BF),
            pltpu.VMEM((6, LINE, rows, GROUP, length), BF),
            pltpu.VMEM((6, GROUP, piece, C), BF),
            pltpu.VMEM((6, GROUP, piece, C), BF),
            pltpu.VMEM((6, pairs, GROUP, GROUP, length), BF),
            pltpu.VMEM((6, pairs, GROUP, GROUP, length), BF),
            pltpu.VMEM((GROUP * (piece + 1), C), FL),
            pltpu.VMEM((GROUP * GROUP, GROUP * GROUP), BF),
            pltpu.VMEM(pair_input.shape, BF),
            pltpu.VMEM(pair_input.shape, BF),
            pltpu.VMEM((SIDE, SIDE, GROWS, C), BF),
            pltpu.VMEM((LINE, SIDE, GROWS, C), BF),
            pltpu.VMEM((SIDE, GROWS, C), BF),
            pltpu.VMEM((GROUP, GROWS, C), BF),
            pltpu.VMEM((GROWS, C), BF),
            pltpu.VMEM((SIDE, GROWS, C), BF),
            pltpu.VMEM((SIDE, SIDE, GROWS, C), BF),
            *[pltpu.VMEM(square, BF)] * 6,
            pltpu.VMEM((LINE * GROUP, length), FL),
            pltpu.VMEM(held, FL),
            pltpu.VMEM((rows, 1, length), FL),
            pltpu.VMEM(held, BF),
            *[pltpu.VMEM(held, FL)] * 7,
            pltpu.VMEM(held, BF),
            pltpu.VMEM(held, BF),
            pltpu.VMEM((rows, 5 * C, length), BF),
            pltpu.VMEM((5 * C, C), BF),
            pltpu.VMEM((C, 5 * C), BF),
            pltpu.VMEM((C, C), BF),
            pltpu.VMEM((C, C), BF),
            pltpu.VMEM((C, C), FL),
            pltpu.VMEM((C, C), FL),
            pltpu.VMEM((C, C), BF),
            pltpu.VMEM((SIDE * SIDE * GROWS, C), BF),
            sem((6, len(CHUNKS))),
            sem((6, len(CHUNKS))),
            sem((6, len(CHUNKS))),
            sem((6, len(CHUNKS))),
            sem((8,)),
            sem((2, rows)),
        ],
        compiler_params=pltpu.CompilerParams(
            collective_id=0, has_side_effects=True, vmem_limit_bytes=58 * 2**20
        ),
    )(pair_input, gain_in.reshape(1, C), w_in, w_out, product_gain.reshape(1, C), cotangent)
    upd, gp, gwi, gwo, ggi, ggo = pl.pallas_call(
        functools.partial(write, rows),
        out_shape=shapes,
        in_specs=[anywhere] * 6,
        out_specs=[anywhere] * 6,
        scratch_shapes=[pltpu.VMEM(shape.shape, shape.dtype) for shape in shapes]
        + [sem((2 * rows + 4,)), sem((2 * rows + 4,))],
        compiler_params=pltpu.CompilerParams(vmem_limit_bytes=60 * 2**20),
    )(*results)
    return upd, gp, gwi, gwo, ggi.reshape(C), ggo.reshape(C)


def solution(mesh):
    return jax.shard_map(
        on_device,
        mesh=mesh,
        in_specs=(
            P(("crop", "res"), None, None),
            P(),
            P(),
            P(),
            P(),
            P(("crop", "res"), None, None),
        ),
        out_specs=(
            P(("crop", "res"), None, None),
            P(("crop", "res"), None, None),
            P("crop", None),
            P("crop", None),
            P("crop"),
            P("crop"),
        ),
        check_vma=False,
    )
```

```python
import functools

import jax
import jax.numpy as jnp
from jax import lax
from jax.experimental import pallas as pl
from jax.experimental.pallas import tpu as pltpu
from jax.sharding import PartitionSpec as P

EPS = 1e-05
FL = jnp.float32
BF = jnp.bfloat16
C = 128
LINE = 8
GROUP = 2 * LINE
GROWS = 16
SIDE = 7
ROUND = (4, 3, 5, 2, 6, 1, 7)
CHUNKS = ((0, 1), (1, 2), (3, 2))
ALL = range(len(CHUNKS))
LATE = (1, 2, 0)


def dot(a, b, dims=((1,), (0,))):
    return lax.dot_general(a, b, (dims, ((), ())), preferred_element_type=FL)


NT = ((1,), (1,))


def padded(count, tiles):
    return -(-(LINE * count * tiles) // 16) * 16


def sigmoid(x):
    return jax.nn.sigmoid(x)


def kernel(
    rows, length,
    z_ref, gain_in_ref, w_in_ref, w_out_ref, gain_out_ref, cot_ref,
    upd_ref, gp_ref, gwi_ref, gwo_ref, ggi_ref, ggo_ref,
    send1, recv1, send2, recv2, send_w, recv_w, mixed, swap, upd_v, gp_v,
    g_send, g_recv, h_send, h_recv, o_send, c_recv, d_recv,
    left_m, right_m, dprod_m, turned_m, order, order_t, wide,
    zhat, zinv, normed, p_l, s_l, p_r, s_r, s_g, cot_t, upd_t, xn, d_lin, d_proj,
    w_in_t, w_in_p, w_out_t, w_out_p, gain_in_c, gain_out_c, perm, grads,
    send_sem1, recv_sem1, send_sem2, recv_sem2, g_sems, out_sems,
):
    tiles = length // C

    def sizes(chunk):
        first, count = CHUNKS[chunk]
        base = LINE * GROUP * first
        return first, count, padded(count, tiles), LINE * count, base

    me = lax.axis_index("res")
    z = me // GROUP
    y = (me // 2) % LINE
    core = me % 2
    a = y + core * (z - y)
    b = z + core * (y - z)
    step_a = 2 + (GROUP - 2) * core
    step_b = GROUP - (GROUP - 2) * core

    def device(at_a, at_b, at_core):
        return at_a * step_a + at_b * step_b + at_core

    def remote(src, dst, on_send, on_recv, to):
        return pltpu.make_async_remote_copy(
            src_ref=src,
            dst_ref=dst,
            send_sem=on_send,
            recv_sem=on_recv,
            device_id={"res": to},
            device_id_type=pl.DeviceIdType.MESH,
        )

    other = device(a, b, 1 - core)
    barrier = pltpu.get_barrier_semaphore()

    def greet(to):
        pl.semaphore_signal(
            barrier, inc=1, device_id={"res": to}, device_id_type=pl.DeviceIdType.MESH
        )

    greet(other)
    for t in ROUND:
        for at_core in (0, 1):
            greet(device((a + t) % LINE, b, at_core))
            greet(device(a, (b + t) % LINE, at_core))

    def send_rows(stage, chunk):
        first, count = CHUNKS[chunk]
        part = pl.ds(first, count)
        for t in ROUND:
            at_a = (a + t) % LINE
            remote(
                send1.at[stage, at_a, part],
                recv1.at[stage, a, part],
                send_sem1.at[stage, chunk],
                recv_sem1.at[stage, chunk],
                device(at_a, b, core),
            ).start()
        recv1[stage, a, part] = send1[stage, a, part]

    def all_a(stage, chunk):
        first, count = CHUNKS[chunk]
        return remote(
            send1.at[stage, pl.ds(0, LINE - 1), pl.ds(first, count)],
            recv1.at[stage, pl.ds(0, LINE - 1), pl.ds(first, count)],
            send_sem1.at[stage, chunk],
            recv_sem1.at[stage, chunk],
            other,
        )

    def all_b(stage, chunk):
        out, into = pieces(stage, chunk)
        return remote(
            out.at[pl.ds(0, GROUP - 1)],
            into.at[pl.ds(0, GROUP - 1)],
            send_sem2.at[stage, chunk],
            recv_sem2.at[stage, chunk],
            other,
        )

    def pieces(stage, chunk):
        if CHUNKS[chunk][1] == 1:
            return send2.at[stage], recv2.at[stage]
        return send_w.at[stage, chunk - 1], recv_w.at[stage, chunk - 1]

    def swapped(value):
        return dot(swap[...], value.reshape(GROUP * GROUP, length)).astype(BF)

    def place(stage, row, value):
        value = value.astype(BF)
        for at in range(LINE):
            send1[stage, at, row] = value[at * GROUP : (at + 1) * GROUP]

    def relay_rows(stage, chunk):
        first, count, piece, _, _ = sizes(chunk)
        out, into = pieces(stage, chunk)
        stride = piece + 1
        all_a(stage, chunk).wait_recv()
        if count == 2:
            out[...] = swapped(recv1[stage, :, first : first + 2]).reshape(GROUP, GROUP, length)
        else:
            for at in range(LINE):
                block = recv1[stage, at, first].astype(FL)
                for tile in range(tiles):
                    mixed[pl.ds(at * tiles + tile, GROUP, stride=stride), :] = block[
                        :, tile * C : (tile + 1) * C
                    ]
            for q in range(GROUP):
                out[q] = mixed[q * stride : q * stride + piece, :].astype(BF)
        mine = b * 2 + core
        for t in ROUND + (0,):
            at_b = (b + t) % LINE
            for turn in (0, 1):
                if t == 0 and turn == 0:
                    continue
                at_core = (core + turn) % 2
                remote(
                    out.at[at_b * 2 + at_core],
                    into.at[mine],
                    send_sem2.at[stage, chunk],
                    recv_sem2.at[stage, chunk],
                    device(a, at_b, at_core),
                ).start()
        into[mine] = out[mine]

    def take_channel(stage, chunk, into):
        first, count, piece, lot, base = sizes(chunk)
        all_b(stage, chunk).wait_recv()
        if count == 2:
            into[base : base + GROUP * lot, :] = pieces(stage, chunk)[1][...].reshape(
                GROUP * lot, length
            )
            return
        for slot in range(GROUP):
            mixed[slot * piece : (slot + 1) * piece, :] = recv2[stage, slot].astype(FL)
        for at in range(LINE):
            top = base + at * 2 * lot
            for tile in range(tiles):
                both = [
                    mixed[pl.ds((at * 2 + k) * piece + tile, lot, stride=tiles), :]
                    for k in (0, 1)
                ]
                into[top : top + 2 * lot, tile * C : (tile + 1) * C] = (
                    jnp.concatenate(both, axis=0).astype(BF)
                )

    def of(factor, chunk):
        _, _, _, lot, base = sizes(chunk)
        return factor[base : base + GROUP * lot, :]

    def send_channel(stage, chunk, whole):
        _, _, piece, lot, _ = sizes(chunk)
        out, into = pieces(stage, chunk)
        single = CHUNKS[chunk][1] == 1
        if single:
            wide[...] = whole
        else:
            out[...] = whole.astype(BF).reshape(GROUP, GROUP, length)
        for t in ROUND + (0,):
            at_b = (b + t) % LINE
            if single:
                part = wide[pl.ds(pl.multiple_of(at_b * 2 * lot, GROUP), 2 * lot), :]
                for k in (0, 1):
                    for tile in range(tiles):
                        mixed[pl.ds(k * piece + tile, lot, stride=tiles), :] = part[
                            k * lot : (k + 1) * lot, tile * C : (tile + 1) * C
                        ]
            for k in (0, 1):
                if single:
                    out[at_b * 2 + k] = mixed[k * piece : (k + 1) * piece, :].astype(BF)
                to = (at_b * GROUP + y * 2) if k == 0 else (z * GROUP + at_b * 2 + 1)
                copy = remote(
                    out.at[at_b * 2 + k],
                    into.at[(z if k == 0 else y) * 2 + core],
                    send_sem2.at[stage, chunk],
                    recv_sem2.at[stage, chunk],
                    to,
                )
                if t == 0:

                    @pl.when(core == k)
                    def _():
                        into[at_b * 2 + k] = out[at_b * 2 + k]

                    @pl.when(core != k)
                    def _():
                        copy.start()

                else:
                    copy.start()

    def relay_channel(stage, chunk):
        first, count, piece, _, _ = sizes(chunk)
        stride = piece + 1
        all_b(stage, chunk).wait_recv()
        into = pieces(stage, chunk)[1]
        if count == 2:
            send1[stage, :, first : first + 2] = swapped(into[...]).reshape(LINE, 2, GROUP, length)
        else:
            for q in range(GROUP):
                mixed[q * stride : q * stride + piece, :] = into[q].astype(FL)
            for at in range(LINE):
                for tile in range(tiles):
                    send1[stage, at, first, :, tile * C : (tile + 1) * C] = mixed[
                        pl.ds(at * tiles + tile, GROUP, stride=stride), :
                    ].astype(BF)
        send_rows(stage, chunk)

    def take_row(stage, row):
        return jnp.concatenate([recv1[stage, at, row] for at in range(LINE)], axis=0).astype(FL)

    def chunk_rows(chunk):
        first, count = CHUNKS[chunk]
        return range(first, first + count)

    def iota(shape, dim):
        return lax.broadcasted_iota(jnp.int32, shape, dim)

    eye = (iota((C, C), 0) == iota((C, C), 1)).astype(BF)
    q = iota((C, C), 0)
    home = (q >> 4) * step_a + ((q >> 1) & 7) * step_b + (q & 1)
    perm_f = (home == iota((C, C), 1)).astype(FL)
    perm[...] = perm_f.astype(BF)
    def weights(block):
        sort = perm[...] if block < 4 else eye
        cols = slice(block * C, (block + 1) * C)
        w_in_t[cols, :] = dot(sort, w_in_ref[:, cols], NT).astype(BF)
        w_in_p[:, cols] = dot(w_in_ref[:, cols], sort, NT).astype(BF)

    weights(2)
    weights(3)
    gain_in_c[...] = jnp.transpose(jnp.broadcast_to(gain_in_ref[...], (C, C)))

    for chunk in ALL:
        for row in chunk_rows(chunk):
            zt = dot(eye, z_ref[row], NT)
            center = zt - jnp.mean(zt, axis=0, keepdims=True)
            inverse = lax.rsqrt(jnp.mean(center * center, axis=0, keepdims=True) + EPS)
            zh = center * inverse
            zhat[row] = zh
            zinv[row] = inverse
            normed[row] = (zh * gain_in_c[:, :1]).astype(BF)
            proj = dot(w_in_t[2 * C : 4 * C, :], normed[row])
            s_r[row] = sigmoid(proj[C:])
            p_r[row] = proj[:C]
            place(1, row, p_r[row] * s_r[row])
        if chunk == 0:
            pl.semaphore_wait(barrier, 4 * LINE - 3)
        send_rows(1, chunk)
    for block in (0, 1, 4):
        weights(block)
    for chunk in LATE:
        for row in chunk_rows(chunk):
            proj = dot(w_in_t[: 2 * C, :], normed[row])
            s_l[row] = sigmoid(proj[C:])
            p_l[row] = proj[:C]
            place(0, row, p_l[row] * s_l[row])
        send_rows(0, chunk)

    w_out_p[...] = dot(perm[...], w_out_ref[...]).astype(BF)
    w_out_t[...] = jnp.transpose(dot(perm[...], w_out_ref[...])).astype(BF)
    gain_out_c[...] = jnp.broadcast_to(
        jnp.sum(perm_f * gain_out_ref[...], axis=1, keepdims=True), (C, C)
    )
    mixed[...] = jnp.zeros(mixed.shape, FL)
    p = iota((1, GROUP * GROUP), 1)
    turned = (p & (GROUP - 1)) * GROUP + (p >> 4)
    swap[...] = (iota((GROUP * GROUP, GROUP * GROUP), 0) == turned).astype(FL).astype(BF)

    def natural(p):
        count = jnp.full(p.shape, float(CHUNKS[0][1]), FL)
        first = jnp.zeros(p.shape, FL)
        for start, size in CHUNKS[1:]:
            later = p >= LINE * GROUP * start
            count = jnp.where(later, float(size), count)
            first = jnp.where(later, float(start), first)
        pf = p.astype(FL) + 0.5 - first * (LINE * GROUP)
        at_b = jnp.floor(pf / (count * GROUP))
        pf = pf - at_b * (count * GROUP)
        at_core = jnp.floor(pf / (count * LINE))
        pf = pf - at_core * (count * LINE)
        at_a = jnp.floor(pf / count)
        row = pf - 0.5 - at_a * count + first
        at_z = at_b + at_core * (at_a - at_b)
        at_y = at_a + at_core * (at_b - at_a)
        return ((at_z * GROUP + at_y * 2 + at_core) * rows + row + 0.5).astype(jnp.int32)

    order[...] = (iota((length, length), 0) == natural(iota((1, length), 1))).astype(FL).astype(BF)
    order_t[...] = (
        (iota((length, length), 1) == natural(iota((length, 1), 0))).astype(FL).astype(BF)
    )

    for chunk in ALL:
        relay_rows(1, chunk)
    for row in range(rows):
        s_g[row] = sigmoid(dot(w_in_t[4 * C :, :], normed[row]))
    for chunk in LATE:
        relay_rows(0, chunk)
    for row in range(rows):
        cot_t[row] = dot(eye, cot_ref[row], NT)
    for chunk in ALL:
        take_channel(1, chunk, turned_m)
    right_m[...] = dot(order[...], turned_m[...]).astype(BF)
    for chunk in LATE:
        take_channel(0, chunk, left_m)
        send_channel(2, chunk, dot(of(left_m, chunk), right_m[...], NT))

    gg_parts = []

    def middle(chunk):
        all_a(2, chunk).wait_recv()
        gg_out = jnp.zeros((C, C), FL)
        for row in chunk_rows(chunk):
            prod = take_row(2, row)
            center = prod - jnp.mean(prod, axis=0, keepdims=True)
            inverse = lax.rsqrt(jnp.mean(center * center, axis=0, keepdims=True) + EPS)
            xh = center * inverse
            xn[row] = (xh * gain_out_c[:, :1]).astype(BF)
            lin = dot(w_out_t[...], xn[row])
            s = s_g[row]
            upd_t[row] = s * lin
            g = cot_t[row]
            d_lin[row] = (g * s).astype(BF)
            d_proj[row, 4 * C :, :] = (g * lin * s * (1.0 - s)).astype(BF)
            d_xn = dot(w_out_p[...], d_lin[row])
            both = d_xn * xh
            for tile in range(tiles):
                gg_out = gg_out + both[:, tile * C : (tile + 1) * C]
            h = d_xn * gain_out_c[:, :1]
            first = jnp.mean(h, axis=0, keepdims=True)
            second = jnp.mean(h * xh, axis=0, keepdims=True)
            place(3, row, inverse * (h - first - xh * second))
        send_rows(3, chunk)
        gg_parts.append(gg_out)

    def left_back(chunk):
        take_channel(3, chunk, dprod_m)
        send_channel(4, chunk, dot(of(dprod_m, chunk), right_m[...]))

    def right_back(chunk):
        send_channel(5, chunk, dot(of(turned_m, chunk), left_m[...]))

    c0, c1, c2 = LATE
    relay_channel(2, c0)
    relay_channel(2, c1)
    middle(c0)
    relay_channel(2, c2)
    middle(c1)
    relay_rows(3, c0)
    middle(c2)
    relay_rows(3, c1)
    left_back(c0)
    relay_rows(3, c2)
    left_back(c1)
    relay_channel(4, c0)
    left_back(c2)
    turned_m[...] = dot(order_t[...], dprod_m[...], NT).astype(BF)
    right_back(c0)
    relay_channel(4, c1)
    right_back(c1)
    relay_channel(4, c2)
    right_back(c2)
    gg_out = gg_parts[0] + gg_parts[1] + gg_parts[2]
    gw = jnp.zeros((C, C), FL)
    gw_gate = jnp.zeros((C, C), FL)
    for row in range(rows):
        gw = gw + dot(xn[row], d_lin[row], NT)
        gw_gate = gw_gate + dot(normed[row], d_proj[row, 4 * C :, :], NT)
    grads[4 * C : 5 * C, :] = gw_gate.astype(BF)
    grads[5 * C : 6 * C, :] = dot(perm[...], gw.astype(BF)).astype(BF)

    def leave(held, out, which, row):
        return pltpu.make_async_copy(held.at[row], out.at[row], out_sems.at[which, row])

    def write_update(picked):
        for row in picked:
            for tile in range(tiles):
                upd_v[row, tile * C : (tile + 1) * C, :] = jnp.transpose(
                    upd_t[row, :, tile * C : (tile + 1) * C]
                ).astype(BF)
            leave(upd_v, upd_ref, 0, row).start()

    def write_rows(picked):
        for row in picked:
            zh = zhat[row]
            h = p_l[row] * gain_in_c[:, :1]
            first = jnp.mean(h, axis=0, keepdims=True)
            second = jnp.mean(h * zh, axis=0, keepdims=True)
            out = zinv[row] * (h - first - zh * second)
            for tile in range(tiles):
                gp_v[row, tile * C : (tile + 1) * C, :] = jnp.transpose(
                    out[:, tile * C : (tile + 1) * C]
                ).astype(BF)
            leave(gp_v, gp_ref, 1, row).start()

    def factor_back(side, chunk, total):
        p_ref, s_ref = ((p_l, s_l), (p_r, s_r))[side]
        base = side * 2 * C
        all_a(4 + side, chunk).wait_recv()
        for row in chunk_rows(chunk):
            d = take_row(4 + side, row)
            s = s_ref[row]
            d_proj[row, base : base + C, :] = (d * s).astype(BF)
            d_proj[row, base + C : base + 2 * C, :] = (d * p_ref[row] * s * (1.0 - s)).astype(BF)
            total = total + dot(normed[row], d_proj[row, base : base + 2 * C, :], NT)
        return total

    def weights_back(side, total):
        base = side * 2 * C
        total = total.astype(BF)
        grads[base : base + C, :] = dot(total[:, :C], perm[...]).astype(BF)
        grads[base + C : base + 2 * C, :] = dot(total[:, C:], perm[...]).astype(BF)

    total = jnp.zeros((C, 2 * C), FL)
    write_update(range(0, 2))
    total = factor_back(0, c0, total)
    relay_channel(5, c0)
    total = factor_back(0, c1, total)
    relay_channel(5, c1)
    total = factor_back(0, c2, total)
    relay_channel(5, c2)
    weights_back(0, total)
    write_update(range(2, rows))
    total = jnp.zeros((C, 2 * C), FL)
    gg_in = jnp.zeros((C, C), FL)
    for chunk in LATE:
        total = factor_back(1, chunk, total)
        for row in chunk_rows(chunk):
            d_normed = dot(w_in_p[...], d_proj[row])
            p_l[row] = d_normed
            both = d_normed * zhat[row]
            for tile in range(tiles):
                gg_in = gg_in + both[:, tile * C : (tile + 1) * C]
        if chunk != c2:
            write_rows(chunk_rows(chunk))
    weights_back(1, total)

    gg_in = jnp.sum(jnp.transpose(gg_in), axis=0, keepdims=True)
    gg_out = jnp.sum(jnp.transpose(gg_out), axis=0, keepdims=True)
    gg_out = dot(jnp.broadcast_to(gg_out, (GROWS, C)).astype(BF), perm[...])
    line = iota((GROWS, C), 0)
    grads[6 * C :, :] = jnp.where(line == 0, jnp.broadcast_to(gg_in, (GROWS, C)), gg_out).astype(BF)

    def both_ways(u, v):
        return v + core * (u - v), u + core * (v - u)

    for u in range(SIDE):
        for v in range(SIDE):
            at = (u * SIDE + v) * GROWS
            g_send[both_ways(u, v)] = grads[at : at + GROWS, :]

    in_a = a < SIDE
    in_b = b < SIDE
    owner = jnp.logical_and(in_a, in_b)
    for t in ROUND:
        at_a = (a + t) % LINE

        @pl.when(at_a < SIDE)
        def _():
            remote(
                g_send.at[at_a], g_recv.at[a], g_sems.at[0], g_sems.at[1], device(at_a, b, core)
            ).start()

    def some(ref, count, on_send, on_recv):
        return remote(ref.at[pl.ds(0, count)], ref.at[pl.ds(0, count)], on_send, on_recv, other)

    write_rows(chunk_rows(c2))
    mine = b * 2 + core

    @pl.when(in_a)
    def _():
        g_recv[a] = g_send[a]
        some(g_recv, LINE - 1, g_sems.at[0], g_sems.at[1]).wait_recv()
        h_send[...] = jnp.sum(g_recv[...].astype(FL), axis=0).astype(BF)
        for t in ROUND + (0,):
            at_b = (b + t) % LINE
            for turn in (0, 1):
                if t == 0 and turn == 0:
                    continue
                at_core = (core + turn) % 2

                @pl.when(at_b < SIDE)
                def _():
                    remote(
                        h_send.at[at_b],
                        h_recv.at[mine],
                        g_sems.at[2],
                        g_sems.at[3],
                        device(a, at_b, at_core),
                    ).start()


    @pl.when(owner)
    def _():
        h_recv[mine] = h_send[b]
        some(h_recv, GROUP - 1, g_sems.at[2], g_sems.at[3]).wait_recv()
        total = jnp.sum(h_recv[...].astype(FL), axis=0) * (1.0 / length)
        o_send[...] = total.astype(BF)
        for t in ROUND:
            remote(
                o_send, c_recv.at[b], g_sems.at[4], g_sems.at[5], device(a, (b + t) % LINE, core)
            ).start()
        c_recv[b] = o_send[...]


    @pl.when(in_a)
    def _():
        @pl.when(in_b)
        def _():
            some(c_recv, SIDE - 1, g_sems.at[4], g_sems.at[5]).wait_recv()

        @pl.when(jnp.logical_not(in_b))
        def _():
            some(c_recv, SIDE, g_sems.at[4], g_sems.at[5]).wait_recv()

        for t in ROUND:
            remote(
                c_recv, d_recv.at[a], g_sems.at[6], g_sems.at[7], device((a + t) % LINE, b, core)
            ).start()
        d_recv[a] = c_recv[...]
        some(d_recv, SIDE - 1, g_sems.at[6], g_sems.at[7]).wait_recv()

    @pl.when(jnp.logical_not(in_a))
    def _():
        some(d_recv, SIDE, g_sems.at[6], g_sems.at[7]).wait_recv()

    per = C // GROWS
    for u in range(SIDE):
        for v in range(SIDE):
            block, at = divmod(u * SIDE + v, per)
            value = d_recv[both_ways(u, v)].astype(FL)
            at = at * GROWS
            if block < 5:
                gwi_ref[at : at + GROWS, block * C : (block + 1) * C] = value
            elif block == 5:
                gwo_ref[at : at + GROWS, :] = value
            else:
                ggi_ref[...] = value[0:1]
                ggo_ref[...] = value[1:2]

    @pl.when(in_a)
    def _():
        some(g_send, SIDE - 1, g_sems.at[0], g_sems.at[1]).wait_send()
        some(g_recv, LINE - 1, g_sems.at[6], g_sems.at[7]).wait_send()

        @pl.when(in_b)
        def _():
            some(h_recv, GROUP - 3, g_sems.at[2], g_sems.at[3]).wait_send()
            some(h_recv, LINE - 1, g_sems.at[4], g_sems.at[5]).wait_send()

        @pl.when(jnp.logical_not(in_b))
        def _():
            some(h_recv, GROUP - 2, g_sems.at[2], g_sems.at[3]).wait_send()

    @pl.when(jnp.logical_not(in_a))
    def _():
        some(g_send, SIDE, g_sems.at[0], g_sems.at[1]).wait_send()

    for stage in range(6):
        for chunk in ALL:
            all_a(stage, chunk).wait_send()
            all_b(stage, chunk).wait_send()
    for row in range(rows):
        leave(upd_v, upd_ref, 0, row).wait()
        leave(gp_v, gp_ref, 1, row).wait()


def write(rows, *refs):
    into, out = refs[-2:]
    pairs = []
    for src, held, dst in zip(refs[:6], refs[12:18], refs[6:12]):
        if len(src.shape) == 3:
            pairs += [(src.at[row], held.at[row], dst.at[row]) for row in range(rows)]
        else:
            pairs.append((src, held, dst))
    reads = [pltpu.make_async_copy(s, h, into.at[i]) for i, (s, h, _) in enumerate(pairs)]
    writes = [pltpu.make_async_copy(h, d, out.at[i]) for i, (_, h, d) in enumerate(pairs)]
    for copy in reads:
        copy.start()
    for read, copy in zip(reads, writes):
        read.wait()
        copy.start()
    for copy in writes:
        copy.wait()


def on_device(pair_input, gain_in, w_in, w_out, product_gain, cotangent):
    rows, length, width = pair_input.shape
    piece = padded(1, length // C)
    pairs = len(CHUNKS) - 1
    anywhere = pl.BlockSpec(memory_space=pl.ANY)
    held = (rows, C, length)
    square = (length, length)
    vmem = pl.BlockSpec(memory_space=pltpu.VMEM)
    sem = pltpu.SemaphoreType.DMA
    shapes = (
        jax.ShapeDtypeStruct(pair_input.shape, BF),
        jax.ShapeDtypeStruct(pair_input.shape, BF),
        jax.ShapeDtypeStruct(w_in.shape, FL),
        jax.ShapeDtypeStruct(w_out.shape, FL),
        jax.ShapeDtypeStruct((1, C), FL),
        jax.ShapeDtypeStruct((1, C), FL),
    )
    results = pl.pallas_call(
        functools.partial(kernel, rows, length),
        out_shape=shapes,
        in_specs=[vmem] * 6,
        out_specs=[anywhere] * 2 + [vmem] * 4,
        scratch_shapes=[
            pltpu.VMEM((6, LINE, rows, GROUP, length), BF),
            pltpu.VMEM((6, LINE, rows, GROUP, length), BF),
            pltpu.VMEM((6, GROUP, piece, C), BF),
            pltpu.VMEM((6, GROUP, piece, C), BF),
            pltpu.VMEM((6, pairs, GROUP, GROUP, length), BF),
            pltpu.VMEM((6, pairs, GROUP, GROUP, length), BF),
            pltpu.VMEM((GROUP * (piece + 1), C), FL),
            pltpu.VMEM((GROUP * GROUP, GROUP * GROUP), BF),
            pltpu.VMEM(pair_input.shape, BF),
            pltpu.VMEM(pair_input.shape, BF),
            pltpu.VMEM((SIDE, SIDE, GROWS, C), BF),
            pltpu.VMEM((LINE, SIDE, GROWS, C), BF),
            pltpu.VMEM((SIDE, GROWS, C), BF),
            pltpu.VMEM((GROUP, GROWS, C), BF),
            pltpu.VMEM((GROWS, C), BF),
            pltpu.VMEM((SIDE, GROWS, C), BF),
            pltpu.VMEM((SIDE, SIDE, GROWS, C), BF),
            *[pltpu.VMEM(square, BF)] * 6,
            pltpu.VMEM((LINE * GROUP, length), FL),
            pltpu.VMEM(held, FL),
            pltpu.VMEM((rows, 1, length), FL),
            pltpu.VMEM(held, BF),
            *[pltpu.VMEM(held, FL)] * 7,
            pltpu.VMEM(held, BF),
            pltpu.VMEM(held, BF),
            pltpu.VMEM((rows, 5 * C, length), BF),
            pltpu.VMEM((5 * C, C), BF),
            pltpu.VMEM((C, 5 * C), BF),
            pltpu.VMEM((C, C), BF),
            pltpu.VMEM((C, C), BF),
            pltpu.VMEM((C, C), FL),
            pltpu.VMEM((C, C), FL),
            pltpu.VMEM((C, C), BF),
            pltpu.VMEM((SIDE * SIDE * GROWS, C), BF),
            sem((6, len(CHUNKS))),
            sem((6, len(CHUNKS))),
            sem((6, len(CHUNKS))),
            sem((6, len(CHUNKS))),
            sem((8,)),
            sem((2, rows)),
        ],
        compiler_params=pltpu.CompilerParams(
            collective_id=0, has_side_effects=True, vmem_limit_bytes=58 * 2**20
        ),
    )(pair_input, gain_in.reshape(1, C), w_in, w_out, product_gain.reshape(1, C), cotangent)
    upd, gp, gwi, gwo, ggi, ggo = pl.pallas_call(
        functools.partial(write, rows),
        out_shape=shapes,
        in_specs=[anywhere] * 6,
        out_specs=[anywhere] * 6,
        scratch_shapes=[pltpu.VMEM(shape.shape, shape.dtype) for shape in shapes]
        + [sem((2 * rows + 4,)), sem((2 * rows + 4,))],
        compiler_params=pltpu.CompilerParams(vmem_limit_bytes=60 * 2**20),
    )(*results)
    return upd, gp, gwi, gwo, ggi.reshape(C), ggo.reshape(C)


def solution(mesh):
    return jax.shard_map(
        on_device,
        mesh=mesh,
        in_specs=(
            P(("crop", "res"), None, None),
            P(),
            P(),
            P(),
            P(),
            P(("crop", "res"), None, None),
        ),
        out_specs=(
            P(("crop", "res"), None, None),
            P(("crop", "res"), None, None),
            P("crop", None),
            P("crop", None),
            P("crop"),
            P("crop"),
        ),
        check_vma=False,
    )
```

```python
import functools

import jax
import jax.numpy as jnp
from jax import lax
from jax.experimental import pallas as pl
from jax.experimental.pallas import tpu as pltpu
from jax.sharding import PartitionSpec as P

EPS = 1e-05
FL = jnp.float32
BF = jnp.bfloat16
C = 128
LINE = 8
GROUP = 2 * LINE
GROWS = 16
SIDE = 7
ROUND = (4, 3, 5, 2, 6, 1, 7)
CHUNKS = ((0, 1), (1, 2), (3, 2))
ALL = range(len(CHUNKS))
LATE = (1, 2, 0)


def dot(a, b, dims=((1,), (0,))):
    return lax.dot_general(a, b, (dims, ((), ())), preferred_element_type=FL)


NT = ((1,), (1,))


def padded(count, tiles):
    return -(-(LINE * count * tiles) // 16) * 16


def sigmoid(x):
    return jax.nn.sigmoid(x)


def kernel(
    rows, length,
    z_ref, gain_in_ref, w_in_ref, w_out_ref, gain_out_ref, cot_ref,
    upd_ref, gp_ref, gwi_ref, gwo_ref, ggi_ref, ggo_ref,
    send1, recv1, send2, recv2, send_w, recv_w, mixed, swap, upd_v, gp_v,
    g_send, g_recv, h_send, h_recv, o_send, c_recv, d_recv,
    left_m, right_m, dprod_m, turned_m, order, order_t, wide,
    zhat, zinv, normed, p_l, s_l, p_r, s_r, s_g, cot_t, upd_t, xn, d_lin, d_proj,
    w_in_t, w_in_p, w_out_t, w_out_p, gain_in_c, gain_out_c, perm, grads,
    send_sem1, recv_sem1, send_sem2, recv_sem2, g_sems, out_sems,
):
    tiles = length // C

    def sizes(chunk):
        first, count = CHUNKS[chunk]
        base = LINE * GROUP * first
        return first, count, padded(count, tiles), LINE * count, base

    me = lax.axis_index("res")
    z = me // GROUP
    y = (me // 2) % LINE
    core = me % 2
    a = y + core * (z - y)
    b = z + core * (y - z)
    step_a = 2 + (GROUP - 2) * core
    step_b = GROUP - (GROUP - 2) * core

    def device(at_a, at_b, at_core):
        return at_a * step_a + at_b * step_b + at_core

    def remote(src, dst, on_send, on_recv, to):
        return pltpu.make_async_remote_copy(
            src_ref=src,
            dst_ref=dst,
            send_sem=on_send,
            recv_sem=on_recv,
            device_id={"res": to},
            device_id_type=pl.DeviceIdType.MESH,
        )

    other = device(a, b, 1 - core)
    barrier = pltpu.get_barrier_semaphore()

    def greet(to):
        pl.semaphore_signal(
            barrier, inc=1, device_id={"res": to}, device_id_type=pl.DeviceIdType.MESH
        )

    greet(other)
    for t in ROUND:
        for at_core in (0, 1):
            greet(device((a + t) % LINE, b, at_core))
            greet(device(a, (b + t) % LINE, at_core))

    def send_rows(stage, chunk):
        first, count = CHUNKS[chunk]
        part = pl.ds(first, count)
        for t in ROUND:
            at_a = (a + t) % LINE
            remote(
                send1.at[stage, at_a, part],
                recv1.at[stage, a, part],
                send_sem1.at[stage, chunk],
                recv_sem1.at[stage, chunk],
                device(at_a, b, core),
            ).start()
        recv1[stage, a, part] = send1[stage, a, part]

    def all_a(stage, chunk):
        first, count = CHUNKS[chunk]
        return remote(
            send1.at[stage, pl.ds(0, LINE - 1), pl.ds(first, count)],
            recv1.at[stage, pl.ds(0, LINE - 1), pl.ds(first, count)],
            send_sem1.at[stage, chunk],
            recv_sem1.at[stage, chunk],
            other,
        )

    def all_b(stage, chunk):
        out, into = pieces(stage, chunk)
        return remote(
            out.at[pl.ds(0, GROUP - 1)],
            into.at[pl.ds(0, GROUP - 1)],
            send_sem2.at[stage, chunk],
            recv_sem2.at[stage, chunk],
            other,
        )

    def pieces(stage, chunk):
        if CHUNKS[chunk][1] == 1:
            return send2.at[stage], recv2.at[stage]
        return send_w.at[stage, chunk - 1], recv_w.at[stage, chunk - 1]

    def swapped(value):
        return dot(swap[...], value.reshape(GROUP * GROUP, length)).astype(BF)

    def place(stage, row, value):
        value = value.astype(BF)
        for at in range(LINE):
            send1[stage, at, row] = value[at * GROUP : (at + 1) * GROUP]

    def relay_rows(stage, chunk):
        first, count, piece, _, _ = sizes(chunk)
        out, into = pieces(stage, chunk)
        stride = piece + 1
        all_a(stage, chunk).wait_recv()
        if count == 2:
            out[...] = swapped(recv1[stage, :, first : first + 2]).reshape(GROUP, GROUP, length)
        else:
            for at in range(LINE):
                block = recv1[stage, at, first].astype(FL)
                for tile in range(tiles):
                    mixed[pl.ds(at * tiles + tile, GROUP, stride=stride), :] = block[
                        :, tile * C : (tile + 1) * C
                    ]
            for q in range(GROUP):
                out[q] = mixed[q * stride : q * stride + piece, :].astype(BF)
        mine = b * 2 + core
        for t in ROUND + (0,):
            at_b = (b + t) % LINE
            for turn in (0, 1):
                if t == 0 and turn == 0:
                    continue
                at_core = (core + turn) % 2
                remote(
                    out.at[at_b * 2 + at_core],
                    into.at[mine],
                    send_sem2.at[stage, chunk],
                    recv_sem2.at[stage, chunk],
                    device(a, at_b, at_core),
                ).start()
        into[mine] = out[mine]

    def take_channel(stage, chunk, into):
        first, count, piece, lot, base = sizes(chunk)
        all_b(stage, chunk).wait_recv()
        if count == 2:
            into[base : base + GROUP * lot, :] = pieces(stage, chunk)[1][...].reshape(
                GROUP * lot, length
            )
            return
        for slot in range(GROUP):
            mixed[slot * piece : (slot + 1) * piece, :] = recv2[stage, slot].astype(FL)
        for at in range(LINE):
            top = base + at * 2 * lot
            for tile in range(tiles):
                both = [
                    mixed[pl.ds((at * 2 + k) * piece + tile, lot, stride=tiles), :]
                    for k in (0, 1)
                ]
                into[top : top + 2 * lot, tile * C : (tile + 1) * C] = (
                    jnp.concatenate(both, axis=0).astype(BF)
                )

    def of(factor, chunk):
        _, _, _, lot, base = sizes(chunk)
        return factor[base : base + GROUP * lot, :]

    def send_channel(stage, chunk, whole):
        _, _, piece, lot, _ = sizes(chunk)
        out, into = pieces(stage, chunk)
        single = CHUNKS[chunk][1] == 1
        if single:
            wide[...] = whole
        else:
            out[...] = whole.astype(BF).reshape(GROUP, GROUP, length)
        for t in ROUND + (0,):
            at_b = (b + t) % LINE
            if single:
                part = wide[pl.ds(pl.multiple_of(at_b * 2 * lot, GROUP), 2 * lot), :]
                for k in (0, 1):
                    for tile in range(tiles):
                        mixed[pl.ds(k * piece + tile, lot, stride=tiles), :] = part[
                            k * lot : (k + 1) * lot, tile * C : (tile + 1) * C
                        ]
            for k in (0, 1):
                if single:
                    out[at_b * 2 + k] = mixed[k * piece : (k + 1) * piece, :].astype(BF)
                to = (at_b * GROUP + y * 2) if k == 0 else (z * GROUP + at_b * 2 + 1)
                copy = remote(
                    out.at[at_b * 2 + k],
                    into.at[(z if k == 0 else y) * 2 + core],
                    send_sem2.at[stage, chunk],
                    recv_sem2.at[stage, chunk],
                    to,
                )
                if t == 0:

                    @pl.when(core == k)
                    def _():
                        into[at_b * 2 + k] = out[at_b * 2 + k]

                    @pl.when(core != k)
                    def _():
                        copy.start()

                else:
                    copy.start()

    def relay_channel(stage, chunk):
        first, count, piece, _, _ = sizes(chunk)
        stride = piece + 1
        all_b(stage, chunk).wait_recv()
        into = pieces(stage, chunk)[1]
        if count == 2:
            send1[stage, :, first : first + 2] = swapped(into[...]).reshape(LINE, 2, GROUP, length)
        else:
            for q in range(GROUP):
                mixed[q * stride : q * stride + piece, :] = into[q].astype(FL)
            for at in range(LINE):
                for tile in range(tiles):
                    send1[stage, at, first, :, tile * C : (tile + 1) * C] = mixed[
                        pl.ds(at * tiles + tile, GROUP, stride=stride), :
                    ].astype(BF)
        send_rows(stage, chunk)

    def take_row(stage, row):
        return jnp.concatenate([recv1[stage, at, row] for at in range(LINE)], axis=0).astype(FL)

    def chunk_rows(chunk):
        first, count = CHUNKS[chunk]
        return range(first, first + count)

    def iota(shape, dim):
        return lax.broadcasted_iota(jnp.int32, shape, dim)

    eye = (iota((C, C), 0) == iota((C, C), 1)).astype(BF)
    q = iota((C, C), 0)
    home = (q >> 4) * step_a + ((q >> 1) & 7) * step_b + (q & 1)
    perm_f = (home == iota((C, C), 1)).astype(FL)
    perm[...] = perm_f.astype(BF)
    def weights(block):
        sort = perm[...] if block < 4 else eye
        cols = slice(block * C, (block + 1) * C)
        w_in_t[cols, :] = dot(sort, w_in_ref[:, cols], NT).astype(BF)
        w_in_p[:, cols] = dot(w_in_ref[:, cols], sort, NT).astype(BF)

    weights(2)
    weights(3)
    gain_in_c[...] = jnp.transpose(jnp.broadcast_to(gain_in_ref[...], (C, C)))

    for chunk in ALL:
        for row in chunk_rows(chunk):
            zt = dot(eye, z_ref[row], NT)
            center = zt - jnp.mean(zt, axis=0, keepdims=True)
            inverse = lax.rsqrt(jnp.mean(center * center, axis=0, keepdims=True) + EPS)
            zh = center * inverse
            zhat[row] = zh
            zinv[row] = inverse
            normed[row] = (zh * gain_in_c[:, :1]).astype(BF)
            proj = dot(w_in_t[2 * C : 4 * C, :], normed[row])
            s_r[row] = sigmoid(proj[C:])
            p_r[row] = proj[:C]
            place(1, row, p_r[row] * s_r[row])
        if chunk == 0:
            pl.semaphore_wait(barrier, 4 * LINE - 3)
        send_rows(1, chunk)
    for block in (0, 1, 4):
        weights(block)
    for chunk in LATE:
        for row in chunk_rows(chunk):
            proj = dot(w_in_t[: 2 * C, :], normed[row])
            s_l[row] = sigmoid(proj[C:])
            p_l[row] = proj[:C]
            place(0, row, p_l[row] * s_l[row])
        send_rows(0, chunk)

    w_out_p[...] = dot(perm[...], w_out_ref[...]).astype(BF)
    w_out_t[...] = jnp.transpose(dot(perm[...], w_out_ref[...])).astype(BF)
    gain_out_c[...] = jnp.broadcast_to(
        jnp.sum(perm_f * gain_out_ref[...], axis=1, keepdims=True), (C, C)
    )
    mixed[...] = jnp.zeros(mixed.shape, FL)
    p = iota((1, GROUP * GROUP), 1)
    turned = (p & (GROUP - 1)) * GROUP + (p >> 4)
    swap[...] = (iota((GROUP * GROUP, GROUP * GROUP), 0) == turned).astype(FL).astype(BF)

    def natural(p):
        count = jnp.full(p.shape, float(CHUNKS[0][1]), FL)
        first = jnp.zeros(p.shape, FL)
        for start, size in CHUNKS[1:]:
            later = p >= LINE * GROUP * start
            count = jnp.where(later, float(size), count)
            first = jnp.where(later, float(start), first)
        pf = p.astype(FL) + 0.5 - first * (LINE * GROUP)
        at_b = jnp.floor(pf / (count * GROUP))
        pf = pf - at_b * (count * GROUP)
        at_core = jnp.floor(pf / (count * LINE))
        pf = pf - at_core * (count * LINE)
        at_a = jnp.floor(pf / count)
        row = pf - 0.5 - at_a * count + first
        at_z = at_b + at_core * (at_a - at_b)
        at_y = at_a + at_core * (at_b - at_a)
        return ((at_z * GROUP + at_y * 2 + at_core) * rows + row + 0.5).astype(jnp.int32)

    order[...] = (iota((length, length), 0) == natural(iota((1, length), 1))).astype(FL).astype(BF)
    order_t[...] = (
        (iota((length, length), 1) == natural(iota((length, 1), 0))).astype(FL).astype(BF)
    )

    for chunk in ALL:
        relay_rows(1, chunk)
    for chunk in LATE:
        relay_rows(0, chunk)
    for row in range(rows):
        s_g[row] = sigmoid(dot(w_in_t[4 * C :, :], normed[row]))
        cot_t[row] = dot(eye, cot_ref[row], NT)
    for chunk in ALL:
        take_channel(1, chunk, turned_m)
    right_m[...] = dot(order[...], turned_m[...]).astype(BF)
    for chunk in LATE:
        take_channel(0, chunk, left_m)
        send_channel(2, chunk, dot(of(left_m, chunk), right_m[...], NT))

    gg_parts = []

    def middle(chunk):
        all_a(2, chunk).wait_recv()
        gg_out = jnp.zeros((C, C), FL)
        for row in chunk_rows(chunk):
            prod = take_row(2, row)
            center = prod - jnp.mean(prod, axis=0, keepdims=True)
            inverse = lax.rsqrt(jnp.mean(center * center, axis=0, keepdims=True) + EPS)
            xh = center * inverse
            xn[row] = (xh * gain_out_c[:, :1]).astype(BF)
            lin = dot(w_out_t[...], xn[row])
            s = s_g[row]
            upd_t[row] = s * lin
            g = cot_t[row]
            d_lin[row] = (g * s).astype(BF)
            d_proj[row, 4 * C :, :] = (g * lin * s * (1.0 - s)).astype(BF)
            d_xn = dot(w_out_p[...], d_lin[row])
            both = d_xn * xh
            for tile in range(tiles):
                gg_out = gg_out + both[:, tile * C : (tile + 1) * C]
            h = d_xn * gain_out_c[:, :1]
            first = jnp.mean(h, axis=0, keepdims=True)
            second = jnp.mean(h * xh, axis=0, keepdims=True)
            place(3, row, inverse * (h - first - xh * second))
        send_rows(3, chunk)
        gg_parts.append(gg_out)

    def left_back(chunk):
        take_channel(3, chunk, dprod_m)
        send_channel(4, chunk, dot(of(dprod_m, chunk), right_m[...]))

    def right_back(chunk):
        send_channel(5, chunk, dot(of(turned_m, chunk), left_m[...]))

    c0, c1, c2 = LATE
    relay_channel(2, c0)
    relay_channel(2, c1)
    middle(c0)
    relay_channel(2, c2)
    middle(c1)
    relay_rows(3, c0)
    middle(c2)
    relay_rows(3, c1)
    left_back(c0)
    relay_rows(3, c2)
    left_back(c1)
    relay_channel(4, c0)
    left_back(c2)
    turned_m[...] = dot(order_t[...], dprod_m[...], NT).astype(BF)
    right_back(c0)
    relay_channel(4, c1)
    right_back(c1)
    relay_channel(4, c2)
    right_back(c2)
    gg_out = gg_parts[0] + gg_parts[1] + gg_parts[2]
    gw = jnp.zeros((C, C), FL)
    gw_gate = jnp.zeros((C, C), FL)
    for row in range(rows):
        gw = gw + dot(xn[row], d_lin[row], NT)
        gw_gate = gw_gate + dot(normed[row], d_proj[row, 4 * C :, :], NT)
    grads[4 * C : 5 * C, :] = gw_gate.astype(BF)
    grads[5 * C : 6 * C, :] = dot(perm[...], gw.astype(BF)).astype(BF)

    def leave(held, out, which, row):
        return pltpu.make_async_copy(held.at[row], out.at[row], out_sems.at[which, row])

    def write_update(picked):
        for row in picked:
            for tile in range(tiles):
                upd_v[row, tile * C : (tile + 1) * C, :] = jnp.transpose(
                    upd_t[row, :, tile * C : (tile + 1) * C]
                ).astype(BF)
            leave(upd_v, upd_ref, 0, row).start()

    def write_rows(picked):
        for row in picked:
            zh = zhat[row]
            h = p_l[row] * gain_in_c[:, :1]
            first = jnp.mean(h, axis=0, keepdims=True)
            second = jnp.mean(h * zh, axis=0, keepdims=True)
            out = zinv[row] * (h - first - zh * second)
            for tile in range(tiles):
                gp_v[row, tile * C : (tile + 1) * C, :] = jnp.transpose(
                    out[:, tile * C : (tile + 1) * C]
                ).astype(BF)
            leave(gp_v, gp_ref, 1, row).start()

    def factor_back(side, chunk, total):
        p_ref, s_ref = ((p_l, s_l), (p_r, s_r))[side]
        base = side * 2 * C
        all_a(4 + side, chunk).wait_recv()
        for row in chunk_rows(chunk):
            d = take_row(4 + side, row)
            s = s_ref[row]
            d_proj[row, base : base + C, :] = (d * s).astype(BF)
            d_proj[row, base + C : base + 2 * C, :] = (d * p_ref[row] * s * (1.0 - s)).astype(BF)
            total = total + dot(normed[row], d_proj[row, base : base + 2 * C, :], NT)
        return total

    def weights_back(side, total):
        base = side * 2 * C
        total = total.astype(BF)
        grads[base : base + C, :] = dot(total[:, :C], perm[...]).astype(BF)
        grads[base + C : base + 2 * C, :] = dot(total[:, C:], perm[...]).astype(BF)

    total = jnp.zeros((C, 2 * C), FL)
    write_update(range(0, 2))
    total = factor_back(0, c0, total)
    relay_channel(5, c0)
    total = factor_back(0, c1, total)
    relay_channel(5, c1)
    total = factor_back(0, c2, total)
    relay_channel(5, c2)
    weights_back(0, total)
    write_update(range(2, rows))
    total = jnp.zeros((C, 2 * C), FL)
    gg_in = jnp.zeros((C, C), FL)
    for chunk in LATE:
        total = factor_back(1, chunk, total)
        for row in chunk_rows(chunk):
            d_normed = dot(w_in_p[...], d_proj[row])
            p_l[row] = d_normed
            both = d_normed * zhat[row]
            for tile in range(tiles):
                gg_in = gg_in + both[:, tile * C : (tile + 1) * C]
        if chunk != c2:
            write_rows(chunk_rows(chunk))
    weights_back(1, total)

    gg_in = jnp.sum(jnp.transpose(gg_in), axis=0, keepdims=True)
    gg_out = jnp.sum(jnp.transpose(gg_out), axis=0, keepdims=True)
    gg_out = dot(jnp.broadcast_to(gg_out, (GROWS, C)).astype(BF), perm[...])
    line = iota((GROWS, C), 0)
    grads[6 * C :, :] = jnp.where(line == 0, jnp.broadcast_to(gg_in, (GROWS, C)), gg_out).astype(BF)

    def both_ways(u, v):
        return v + core * (u - v), u + core * (v - u)

    for u in range(SIDE):
        for v in range(SIDE):
            at = (u * SIDE + v) * GROWS
            g_send[both_ways(u, v)] = grads[at : at + GROWS, :]

    in_a = a < SIDE
    in_b = b < SIDE
    owner = jnp.logical_and(in_a, in_b)
    for t in ROUND:
        at_a = (a + t) % LINE

        @pl.when(at_a < SIDE)
        def _():
            remote(
                g_send.at[at_a], g_recv.at[a], g_sems.at[0], g_sems.at[1], device(at_a, b, core)
            ).start()

    def some(ref, count, on_send, on_recv):
        return remote(ref.at[pl.ds(0, count)], ref.at[pl.ds(0, count)], on_send, on_recv, other)

    write_rows(chunk_rows(c2))
    mine = b * 2 + core

    @pl.when(in_a)
    def _():
        g_recv[a] = g_send[a]
        some(g_recv, LINE - 1, g_sems.at[0], g_sems.at[1]).wait_recv()
        h_send[...] = jnp.sum(g_recv[...].astype(FL), axis=0).astype(BF)
        for t in ROUND + (0,):
            at_b = (b + t) % LINE
            for turn in (0, 1):
                if t == 0 and turn == 0:
                    continue
                at_core = (core + turn) % 2

                @pl.when(at_b < SIDE)
                def _():
                    remote(
                        h_send.at[at_b],
                        h_recv.at[mine],
                        g_sems.at[2],
                        g_sems.at[3],
                        device(a, at_b, at_core),
                    ).start()


    @pl.when(owner)
    def _():
        h_recv[mine] = h_send[b]
        some(h_recv, GROUP - 1, g_sems.at[2], g_sems.at[3]).wait_recv()
        total = jnp.sum(h_recv[...].astype(FL), axis=0) * (1.0 / length)
        o_send[...] = total.astype(BF)
        for t in ROUND:
            remote(
                o_send, c_recv.at[b], g_sems.at[4], g_sems.at[5], device(a, (b + t) % LINE, core)
            ).start()
        c_recv[b] = o_send[...]


    @pl.when(in_a)
    def _():
        @pl.when(in_b)
        def _():
            some(c_recv, SIDE - 1, g_sems.at[4], g_sems.at[5]).wait_recv()

        @pl.when(jnp.logical_not(in_b))
        def _():
            some(c_recv, SIDE, g_sems.at[4], g_sems.at[5]).wait_recv()

        for t in ROUND:
            remote(
                c_recv, d_recv.at[a], g_sems.at[6], g_sems.at[7], device((a + t) % LINE, b, core)
            ).start()
        d_recv[a] = c_recv[...]
        some(d_recv, SIDE - 1, g_sems.at[6], g_sems.at[7]).wait_recv()

    @pl.when(jnp.logical_not(in_a))
    def _():
        some(d_recv, SIDE, g_sems.at[6], g_sems.at[7]).wait_recv()

    per = C // GROWS
    for u in range(SIDE):
        for v in range(SIDE):
            block, at = divmod(u * SIDE + v, per)
            value = d_recv[both_ways(u, v)].astype(FL)
            at = at * GROWS
            if block < 5:
                gwi_ref[at : at + GROWS, block * C : (block + 1) * C] = value
            elif block == 5:
                gwo_ref[at : at + GROWS, :] = value
            else:
                ggi_ref[...] = value[0:1]
                ggo_ref[...] = value[1:2]

    @pl.when(in_a)
    def _():
        some(g_send, SIDE - 1, g_sems.at[0], g_sems.at[1]).wait_send()
        some(g_recv, LINE - 1, g_sems.at[6], g_sems.at[7]).wait_send()

        @pl.when(in_b)
        def _():
            some(h_recv, GROUP - 3, g_sems.at[2], g_sems.at[3]).wait_send()
            some(h_recv, LINE - 1, g_sems.at[4], g_sems.at[5]).wait_send()

        @pl.when(jnp.logical_not(in_b))
        def _():
            some(h_recv, GROUP - 2, g_sems.at[2], g_sems.at[3]).wait_send()

    @pl.when(jnp.logical_not(in_a))
    def _():
        some(g_send, SIDE, g_sems.at[0], g_sems.at[1]).wait_send()

    for stage in range(6):
        for chunk in ALL:
            all_a(stage, chunk).wait_send()
            all_b(stage, chunk).wait_send()
    for row in range(rows):
        leave(upd_v, upd_ref, 0, row).wait()
        leave(gp_v, gp_ref, 1, row).wait()


def write(rows, *refs):
    into, out = refs[-2:]
    pairs = []
    for src, held, dst in zip(refs[:6], refs[12:18], refs[6:12]):
        if len(src.shape) == 3:
            pairs += [(src.at[row], held.at[row], dst.at[row]) for row in range(rows)]
        else:
            pairs.append((src, held, dst))
    reads = [pltpu.make_async_copy(s, h, into.at[i]) for i, (s, h, _) in enumerate(pairs)]
    writes = [pltpu.make_async_copy(h, d, out.at[i]) for i, (_, h, d) in enumerate(pairs)]
    for copy in reads:
        copy.start()
    for read, copy in zip(reads, writes):
        read.wait()
        copy.start()
    for copy in writes:
        copy.wait()


def on_device(pair_input, gain_in, w_in, w_out, product_gain, cotangent):
    rows, length, width = pair_input.shape
    piece = padded(1, length // C)
    pairs = len(CHUNKS) - 1
    anywhere = pl.BlockSpec(memory_space=pl.ANY)
    held = (rows, C, length)
    square = (length, length)
    vmem = pl.BlockSpec(memory_space=pltpu.VMEM)
    sem = pltpu.SemaphoreType.DMA
    shapes = (
        jax.ShapeDtypeStruct(pair_input.shape, BF),
        jax.ShapeDtypeStruct(pair_input.shape, BF),
        jax.ShapeDtypeStruct(w_in.shape, FL),
        jax.ShapeDtypeStruct(w_out.shape, FL),
        jax.ShapeDtypeStruct((1, C), FL),
        jax.ShapeDtypeStruct((1, C), FL),
    )
    results = pl.pallas_call(
        functools.partial(kernel, rows, length),
        out_shape=shapes,
        in_specs=[vmem] * 6,
        out_specs=[anywhere] * 2 + [vmem] * 4,
        scratch_shapes=[
            pltpu.VMEM((6, LINE, rows, GROUP, length), BF),
            pltpu.VMEM((6, LINE, rows, GROUP, length), BF),
            pltpu.VMEM((6, GROUP, piece, C), BF),
            pltpu.VMEM((6, GROUP, piece, C), BF),
            pltpu.VMEM((6, pairs, GROUP, GROUP, length), BF),
            pltpu.VMEM((6, pairs, GROUP, GROUP, length), BF),
            pltpu.VMEM((GROUP * (piece + 1), C), FL),
            pltpu.VMEM((GROUP * GROUP, GROUP * GROUP), BF),
            pltpu.VMEM(pair_input.shape, BF),
            pltpu.VMEM(pair_input.shape, BF),
            pltpu.VMEM((SIDE, SIDE, GROWS, C), BF),
            pltpu.VMEM((LINE, SIDE, GROWS, C), BF),
            pltpu.VMEM((SIDE, GROWS, C), BF),
            pltpu.VMEM((GROUP, GROWS, C), BF),
            pltpu.VMEM((GROWS, C), BF),
            pltpu.VMEM((SIDE, GROWS, C), BF),
            pltpu.VMEM((SIDE, SIDE, GROWS, C), BF),
            *[pltpu.VMEM(square, BF)] * 6,
            pltpu.VMEM((LINE * GROUP, length), FL),
            pltpu.VMEM(held, FL),
            pltpu.VMEM((rows, 1, length), FL),
            pltpu.VMEM(held, BF),
            *[pltpu.VMEM(held, FL)] * 7,
            pltpu.VMEM(held, BF),
            pltpu.VMEM(held, BF),
            pltpu.VMEM((rows, 5 * C, length), BF),
            pltpu.VMEM((5 * C, C), BF),
            pltpu.VMEM((C, 5 * C), BF),
            pltpu.VMEM((C, C), BF),
            pltpu.VMEM((C, C), BF),
            pltpu.VMEM((C, C), FL),
            pltpu.VMEM((C, C), FL),
            pltpu.VMEM((C, C), BF),
            pltpu.VMEM((SIDE * SIDE * GROWS, C), BF),
            sem((6, len(CHUNKS))),
            sem((6, len(CHUNKS))),
            sem((6, len(CHUNKS))),
            sem((6, len(CHUNKS))),
            sem((8,)),
            sem((2, rows)),
        ],
        compiler_params=pltpu.CompilerParams(
            collective_id=0, has_side_effects=True, vmem_limit_bytes=58 * 2**20
        ),
    )(pair_input, gain_in.reshape(1, C), w_in, w_out, product_gain.reshape(1, C), cotangent)
    upd, gp, gwi, gwo, ggi, ggo = pl.pallas_call(
        functools.partial(write, rows),
        out_shape=shapes,
        in_specs=[anywhere] * 6,
        out_specs=[anywhere] * 6,
        scratch_shapes=[pltpu.VMEM(shape.shape, shape.dtype) for shape in shapes]
        + [sem((2 * rows + 4,)), sem((2 * rows + 4,))],
        compiler_params=pltpu.CompilerParams(vmem_limit_bytes=60 * 2**20),
    )(*results)
    return upd, gp, gwi, gwo, ggi.reshape(C), ggo.reshape(C)


def solution(mesh):
    return jax.shard_map(
        on_device,
        mesh=mesh,
        in_specs=(
            P(("crop", "res"), None, None),
            P(),
            P(),
            P(),
            P(),
            P(("crop", "res"), None, None),
        ),
        out_specs=(
            P(("crop", "res"), None, None),
            P(("crop", "res"), None, None),
            P("crop", None),
            P("crop", None),
            P("crop"),
            P("crop"),
        ),
        check_vma=False,
    )
```
